32 devices in a mesh: row: 16 (over z, y, x), col: 2 (over core).
Axes of the slice: x: 2, y: 2, z: 4, core: 2. Of those that a mesh axis runs over, the one named last changes fastest.
Arguments:
- tables: float32 [262144, 1024], P('row', 'col'), may hold values from -3 to 3
- table_moment: float32 [262144, 1024], P('row', 'col'), may hold values from -3.8146973e-05 to 3.8146973e-05
- table_square: float32 [262144, 1024], P('row', 'col'), may hold values from 5.9604643e-13 to 2.3841857e-12
- expert_weight: float32 [8, 1024, 512], P(None, ('row', 'col')), may hold values from -0.1875 to 0.1875
- expert_moment: float32 [8, 1024, 512], P(None, ('row', 'col')), may hold values from -0.00048828125 to 0.00048828125
- expert_square: float32 [8, 1024, 512], P(None, ('row', 'col')), may hold values from 9.765625e-11 to 3.90625e-10
- gate_weight: float32 [5, 1024, 8], P(None, ('row', 'col')), may hold values from -0.1875 to 0.1875
- gate_moment: float32 [5, 1024, 8], P(None, ('row', 'col')), may hold values from -0.00024414062 to 0.00024414062
- gate_square: float32 [5, 1024, 8], P(None, ('row', 'col')), may hold values from 2.4414063e-11 to 9.765625e-11
- tower_weight: float32 [5, 512, 64], P(None, ('row', 'col')), may hold values from -0.5 to 0.5
- tower_moment: float32 [5, 512, 64], P(None, ('row', 'col')), may hold values from -0.00024414062 to 0.00024414062
- tower_square: float32 [5, 512, 64], P(None, ('row', 'col')), may hold values from 2.4414063e-11 to 9.765625e-11
- expert_bias: float32 [8, 512], replicated, may hold values from -1.5 to 1.5
- bias_moment: float32 [8, 512], replicated, may hold values from -0.00048828125 to 0.00048828125
- bias_square: float32 [8, 512], replicated, may hold values from 9.765625e-11 to 3.90625e-10
- head_bias: float32 [5, 65], replicated, may hold values from -1.5 to 1.5
- head_moment: float32 [5, 65], replicated, may hold values from -0.0012207031 to 0.0012207031
- head_square: float32 [5, 65], replicated, may hold values from 6.1035155e-10 to 2.4414062e-09
- tower_output: float32 [5, 64], replicated, may hold values from -1.5 to 1.5
- output_moment: float32 [5, 64], replicated, may hold values from -0.0024414062 to 0.0024414062
- output_square: float32 [5, 64], replicated, may hold values from 2.4414062e-09 to 9.765625e-09
- lookup_ids: int32 [4096, 16, 4], P(('row', 'col')), may hold values from 0 to 262143, as said below
- bag_lengths: int32 [4096, 16], P(('row', 'col')), may hold values from 1 to 4
- sample_counts: int32 [32], P(('row', 'col')), may hold values from 1 to 128, as said below
- labels: int32 [4096, 5], P(('row', 'col')), may hold values 0 or 1
- label_mask: int32 [4096, 5], P(('row', 'col')), may hold values 0 or 1
- sample_weight: float32 [4096], P(('row', 'col')), may hold values from 0.5 to 2
Outputs:
- updated_tables: float32 [262144, 1024], P('row', 'col')
- updated_table_moment: float32 [262144, 1024], P('row', 'col')
- updated_table_square: float32 [262144, 1024], P('row', 'col')
- updated_expert_weight: float32 [8, 1024, 512], P(None, ('row', 'col'))
- updated_expert_moment: float32 [8, 1024, 512], P(None, ('row', 'col'))
- updated_expert_square: float32 [8, 1024, 512], P(None, ('row', 'col'))
- updated_gate_weight: float32 [5, 1024, 8], P(None, ('row', 'col'))
- updated_gate_moment: float32 [5, 1024, 8], P(None, ('row', 'col'))
- updated_gate_square: float32 [5, 1024, 8], P(None, ('row', 'col'))
- updated_tower_weight: float32 [5, 512, 64], P(None, ('row', 'col'))
- updated_tower_moment: float32 [5, 512, 64], P(None, ('row', 'col'))
- updated_tower_square: float32 [5, 512, 64], P(None, ('row', 'col'))
- updated_expert_bias: float32 [8, 512], replicated
- updated_bias_moment: float32 [8, 512], replicated
- updated_bias_square: float32 [8, 512], replicated
- updated_head_bias: float32 [5, 65], replicated
- updated_head_moment: float32 [5, 65], replicated
- updated_head_square: float32 [5, 65], replicated
- updated_tower_output: float32 [5, 64], replicated
- updated_output_moment: float32 [5, 64], replicated
- updated_output_square: float32 [5, 64], replicated
- loss_sum: float32 [], replicated
- weight_total: float32 [], replicated
The draws below stay inside these ranges and needn't reach their ends.
Inputs may be any that keep to these rules, and one draw needn't show every extreme that they name: sample_counts[d] counts the live samples of device d, devices in the order of row, then col; the last device holds exactly 128. `lookup_ids`: the row pieces are the row axis's blocks of 262144 / 16 consecutive rows. In each table, lookup slot j of the i-th sample of a device (i from 0 to 127) lies in row piece (i * 4 + j + s) mod 16, where s depends only on the device and the table.
All inputs are finite; a program needn't handle non-finite values. No bound on the sum of `labels` or of `label_mask` on one device may be relied on, other than what follows from the above.
Results may differ from the reference program's by a relative error of at most 0.0003.
Values sent between devices are 32-bit elements; how exact they have to be, the bound alone decides.
No kernel may reach another device: no remote copies, remote signals or barrier semaphores. Data moves between devices by JAX's collectives and lax.ppermute only.
A program may use at most 704 MiB of HBM per device.

```python
import math
import jax
import jax.numpy as jnp
from jax import lax

TABS = 16
ROWS = 262144
DIM = 64
BAG = 4
EXPERTS = 8
HID = 512
TOWER = 64
TASKS = 5
STEP = 10
SAMP_DEV = 128
SAMPLES = 4096
N_ROW = 16
N_COL = 2
DEVICES = 32


def draw_sample_counts(key, part):
    key = jax.random.fold_in(key, 7)
    device_index = jnp.arange(DEVICES, dtype=jnp.int32)
    row_position = device_index // N_COL
    col_position = device_index % N_COL
    rows_all = DEVICES // N_COL
    base = SAMP_DEV * (rows_all - 1 + row_position) * (1 + N_COL + col_position - (N_COL - 1)) // (2 * (rows_all - 1) * (1 + N_COL))
    jitter = jax.random.randint(key, (DEVICES,), 0, max(SAMP_DEV // 8, 2), dtype=jnp.int32)
    counts = jnp.maximum(base - jitter, 1)
    return jnp.where(device_index == DEVICES - 1, SAMP_DEV, counts).astype(jnp.int32)


def draw_lookup_ids(key, part):
    key = jax.random.fold_in(key, 11)
    key_shift, key_first, key_second = jax.random.split(key, 3)
    rows_piece = ROWS // N_ROW
    sample = jnp.arange(SAMPLES, dtype=jnp.int32)
    device = sample // SAMP_DEV
    local = sample % SAMP_DEV
    shift = jax.random.randint(key_shift, (DEVICES, TABS), 0, N_ROW, dtype=jnp.int32)
    slot = jnp.arange(BAG, dtype=jnp.int32)
    owner = (local[:, None, None] * BAG + slot[None, None, :] + shift[device][:, :, None]) % N_ROW
    first = jax.random.randint(key_first, (SAMPLES, TABS, BAG), 0, rows_piece, dtype=jnp.int32)
    second = jax.random.randint(key_second, (SAMPLES, TABS, BAG), 0, rows_piece, dtype=jnp.int32)
    offset = first * second // rows_piece
    return (owner * rows_piece + offset).astype(jnp.int32)


def set_ends(values, rng, least, high):
    longest = values.shape.index(max(values.shape))
    spots = []
    for shift in (0, 1):
        where = [jax.random.randint(jax.random.fold_in(rng, axis), (), 0, length) for axis, length in enumerate(values.shape)]
        where[longest] = (where[longest] + shift) % values.shape[longest]
        spots.append(tuple(where))
    return values.at[spots[0]].set(least).at[spots[1]].set(high)


def block_scale(stream_key, dims, pieces, smallest, top_value):
    def one(dim, blocks):
        heights = jax.random.uniform(jax.random.fold_in(jax.random.fold_in(stream_key, 6), dim), (blocks,), jnp.float32, smallest / len(pieces), top_value / len(pieces))
        return jnp.repeat(jnp.exp(heights), dims[dim] // blocks).reshape((-1,) + (1,) * (len(dims) - dim - 1))

    factor_of = one(*pieces[0])
    for cut in pieces[1:]:
        factor_of = factor_of * one(*cut)
    return factor_of


def gaussian(key, dims, deviation, most, shards=(), held_as=jnp.bfloat16):
    drawn = jax.random.normal(key, dims, jnp.float32) * deviation
    if len(shards) > 0:
        drawn = block_scale(key, dims, shards, -0.22, 0.18) * drawn
    return jnp.clip(drawn, min=-most, max=most).astype(held_as)


def setup_inputs(seed: int = 0) -> dict:
    streams_of = jax.random.split(jax.random.key(seed), 28)
    tables = gaussian(streams_of[0], (ROWS, TABS * DIM), 0.5, 3.0, ((0, 16), (1, 2)), jnp.float32)
    table_moment = gaussian(streams_of[1], (ROWS, TABS * DIM), (0.111 * 0.1 / SAMPLES), 3.814697265625e-05, ((0, 16), (1, 2)), jnp.float32)
    table_square = jnp.clip(5.960464326965065e-13 + 1.7881392980895194e-12 * jax.random.uniform(streams_of[2], (ROWS, TABS * DIM), jnp.float32) ** block_scale(streams_of[2], (ROWS, TABS * DIM), ((0, 16), (1, 2)), -0.2, 0.2), 5.960464326965065e-13, 2.384185730786026e-12)
    expert_weight = gaussian(streams_of[3], (EXPERTS, TABS * DIM, HID), (TABS * DIM) ** -0.5, 0.1875, ((1, 32),), jnp.float32)
    expert_moment = gaussian(streams_of[4], (EXPERTS, TABS * DIM, HID), (0.111 * 0.02 / SAMPLES ** 0.5), 0.00048828125, ((1, 32),), jnp.float32)
    expert_square = jnp.clip(9.765625114122045e-11 + 2.9296875342366135e-10 * jax.random.uniform(streams_of[5], (EXPERTS, TABS * DIM, HID), jnp.float32) ** block_scale(streams_of[5], (EXPERTS, TABS * DIM, HID), ((1, 32),), -0.2, 0.2), 9.765625114122045e-11, 3.906250045648818e-10)
    gate_weight = gaussian(streams_of[6], (TASKS, TABS * DIM, EXPERTS), (TABS * DIM) ** -0.5, 0.1875, ((1, 32),), jnp.float32)
    gate_moment = gaussian(streams_of[7], (TASKS, TABS * DIM, EXPERTS), (0.111 * 0.01 / SAMPLES ** 0.5), 0.00024414062, ((1, 32),), jnp.float32)
    gate_square = jnp.clip(2.4414062785305113e-11 + 7.324218835591534e-11 * jax.random.uniform(streams_of[8], (TASKS, TABS * DIM, EXPERTS), jnp.float32) ** block_scale(streams_of[8], (TASKS, TABS * DIM, EXPERTS), ((1, 32),), -0.2, 0.2), 2.4414062785305113e-11, 9.765625114122045e-11)
    tower_weight = gaussian(streams_of[9], (TASKS, HID, TOWER), (HID // 4) ** -0.5, 0.5, ((1, 32),), jnp.float32)
    tower_moment = gaussian(streams_of[10], (TASKS, HID, TOWER), (0.111 * 0.01 / SAMPLES ** 0.5), 0.00024414062, ((1, 32),), jnp.float32)
    tower_square = jnp.clip(2.4414062785305113e-11 + 7.324218835591534e-11 * jax.random.uniform(streams_of[11], (TASKS, HID, TOWER), jnp.float32) ** block_scale(streams_of[11], (TASKS, HID, TOWER), ((1, 32),), -0.2, 0.2), 2.4414062785305113e-11, 9.765625114122045e-11)
    expert_bias = gaussian(streams_of[12], (EXPERTS, HID), 0.1, 1.5, (), jnp.float32)
    bias_moment = gaussian(streams_of[13], (EXPERTS, HID), (0.111 * 0.02 / SAMPLES ** 0.5), 0.00048828125, (), jnp.float32)
    bias_square = jnp.clip(jax.random.uniform(streams_of[14], (EXPERTS, HID), jnp.float32, 9.765625114122045e-11, 3.906250045648818e-10), 9.765625114122045e-11, 3.906250045648818e-10)
    head_bias = gaussian(streams_of[15], (TASKS, TOWER + 1), 0.1, 1.5, (), jnp.float32)
    head_moment = gaussian(streams_of[16], (TASKS, TOWER + 1), (0.111 * 0.05 / SAMPLES ** 0.5), 0.0012207031, (), jnp.float32)
    head_square = jnp.clip(jax.random.uniform(streams_of[17], (TASKS, TOWER + 1), jnp.float32, 6.103515470812226e-10, 2.4414061883248905e-09), 6.103515470812226e-10, 2.4414061883248905e-09)
    tower_output = gaussian(streams_of[18], (TASKS, TOWER), (TOWER // 4) ** -0.5, 1.5, (), jnp.float32)
    output_moment = gaussian(streams_of[19], (TASKS, TOWER), (0.111 * 0.1 / SAMPLES ** 0.5), 0.0024414062, (), jnp.float32)
    output_square = jnp.clip(jax.random.uniform(streams_of[20], (TASKS, TOWER), jnp.float32, 2.4414061883248905e-09, 9.765624753299562e-09), 2.4414061883248905e-09, 9.765624753299562e-09)
    lookup_ids = draw_lookup_ids(jax.random.fold_in(streams_of[27], 71), 0)
    bag_lengths = set_ends(jax.random.randint(streams_of[22], (SAMPLES, TABS), 1, BAG + 1), jax.random.fold_in(streams_of[22], 1), 1, BAG).astype(jnp.int32)
    sample_counts = draw_sample_counts(jax.random.fold_in(streams_of[27], 71), 0)
    labels = set_ends((jax.random.randint(streams_of[24], (SAMPLES, TASKS), 0, 2) < 1).astype(jnp.int32), jax.random.fold_in(streams_of[24], 1), 0, 1)
    label_mask = set_ends((jax.random.randint(streams_of[25], (SAMPLES, TASKS), 0, 10) < 7).astype(jnp.int32), jax.random.fold_in(streams_of[25], 1), 0, 1)
    sample_weight = jnp.clip(jnp.exp(math.log(2.0) - 1.3862944 * jax.random.uniform(streams_of[26], (SAMPLES,), jnp.float32) ** block_scale(streams_of[26], (SAMPLES,), ((0, 32),), -0.2, 0.2)), 0.5, 2.0)
    return dict(tables=tables, table_moment=table_moment, table_square=table_square, expert_weight=expert_weight, expert_moment=expert_moment, expert_square=expert_square, gate_weight=gate_weight, gate_moment=gate_moment, gate_square=gate_square, tower_weight=tower_weight, tower_moment=tower_moment, tower_square=tower_square, expert_bias=expert_bias, bias_moment=bias_moment, bias_square=bias_square, head_bias=head_bias, head_moment=head_moment, head_square=head_square, tower_output=tower_output, output_moment=output_moment, output_square=output_square, lookup_ids=lookup_ids, bag_lengths=bag_lengths, sample_counts=sample_counts, labels=labels, label_mask=label_mask, sample_weight=sample_weight)


HIGHEST = lax.Precision.HIGHEST
beta_one = 0.9
beta_two = 0.999
epsilon = 1e-08
decay_rate = 0.01
table_rate = 0.2
dense_rate = 0.02

@jax.custom_vjp
def low(v):
    return lax.optimization_barrier(v.astype(jnp.bfloat16)).astype(jnp.float32)

@jax.custom_vjp
def low_back(v):
    return v

def low_keep(v):
    return (low(v), None)

def low_pass(kept, grad):
    return (grad,)

def back_keep(v):
    return (v, None)

def back_low(kept, grad):
    return (low(grad),)
low.defvjp(low_keep, low_pass)
low_back.defvjp(back_keep, back_low)

def adamw(weight, moment, square, gradient, rate):
    moment_next = beta_one * moment + (1.0 - beta_one) * gradient
    square_next = beta_two * square + (1.0 - beta_two) * gradient * gradient
    moment_hat = moment_next / (1.0 - beta_one ** STEP)
    square_hat = square_next / (1.0 - beta_two ** STEP)
    weight_next = weight - rate * (moment_hat / (jnp.sqrt(square_hat) + epsilon) + decay_rate * weight)
    return (weight_next, moment_next, square_next)

def dense_loss(inputs, expert_weight, expert_bias, gate_weight, tower_weight, head_bias, tower_output, targets, keep):
    preact = jnp.einsum('nk,ekh->enh', inputs, expert_weight, precision=HIGHEST) + expert_bias[:, None, :]
    hidden = jax.nn.gelu(preact)
    gate_probs = jax.nn.softmax(jnp.einsum('nk,tke->tne', inputs, gate_weight, precision=HIGHEST), axis=-1)
    mixed = jnp.einsum('tne,enh->tnh', gate_probs, hidden, precision=HIGHEST)
    inner = jnp.einsum('tnh,thc->tnc', mixed, tower_weight, precision=HIGHEST) + head_bias[:, None, :-1]
    score = jnp.einsum('tnc,tc->tn', jax.nn.gelu(inner), tower_output, precision=HIGHEST) + head_bias[:, -1:]
    return jnp.sum(keep * (jax.nn.softplus(score) - targets * score))

def pool(tables, lookup_ids, use_weight):
    blocks = tables.reshape(ROWS, TABS, DIM)
    table_index = jnp.broadcast_to(jnp.arange(TABS, dtype=jnp.int32)[None, :, None], lookup_ids.shape)
    picked = blocks[lookup_ids, table_index]
    return lax.optimization_barrier(jnp.sum(picked * use_weight[..., None], axis=2)).reshape(lookup_ids.shape[0], -1)

def reference(tables, table_moment, table_square, expert_weight, expert_moment, expert_square, gate_weight, gate_moment, gate_square, tower_weight, tower_moment, tower_square, expert_bias, bias_moment, bias_square, head_bias, head_moment, head_square, tower_output, output_moment, output_square, lookup_ids, bag_lengths, sample_counts, labels, label_mask, sample_weight):
    slots = jnp.arange(SAMPLES, dtype=jnp.int32)
    live = (slots % SAMP_DEV < sample_counts[slots // SAMP_DEV]).astype(jnp.float32)
    keep = (sample_weight[:, None] * label_mask.astype(jnp.float32) * live[:, None]).T
    targets = labels.astype(jnp.float32).T
    position = jnp.arange(BAG, dtype=jnp.int32)
    use_weight = (position[None, None, :] < bag_lengths[:, :, None]).astype(jnp.float32)

    def total(tables, expert_weight, expert_bias, gate_weight, tower_weight, head_bias, tower_output):
        inputs = pool(tables, lookup_ids, use_weight)
        return dense_loss(inputs, expert_weight, expert_bias, gate_weight, tower_weight, head_bias, tower_output, targets, keep)
    loss_sum, pullback = jax.vjp(total, tables, expert_weight, expert_bias, gate_weight, tower_weight, head_bias, tower_output)
    weight_total = jnp.sum(keep)
    grads = pullback(1.0 / weight_total)
    table_index = jnp.broadcast_to(jnp.arange(TABS, dtype=jnp.int32)[None, :, None], lookup_ids.shape)
    hits = jnp.zeros((ROWS, TABS), jnp.float32).at[lookup_ids, table_index].add(use_weight)
    touched = jnp.broadcast_to((hits > 0.0)[:, :, None], (ROWS, TABS, DIM)).reshape(ROWS, TABS * DIM)
    fresh_tab, fresh_mom, fresh_sq = adamw(tables, table_moment, table_square, grads[0], table_rate)
    new_tab = jnp.where(touched, fresh_tab, tables)
    new_mom = jnp.where(touched, fresh_mom, table_moment)
    new_sq = jnp.where(touched, fresh_sq, table_square)
    experts_new = adamw(expert_weight, expert_moment, expert_square, grads[1], dense_rate)
    gates_new = adamw(gate_weight, gate_moment, gate_square, grads[3], dense_rate)
    towers_new = adamw(tower_weight, tower_moment, tower_square, grads[4], dense_rate)
    biases_new = adamw(expert_bias, bias_moment, bias_square, grads[2], dense_rate)
    heads_new = adamw(head_bias, head_moment, head_square, grads[5], dense_rate)
    outputs_new = adamw(tower_output, output_moment, output_square, grads[6], dense_rate)
    return (new_tab, new_mom, new_sq, experts_new[0], experts_new[1], experts_new[2], gates_new[0], gates_new[1], gates_new[2], towers_new[0], towers_new[1], towers_new[2], biases_new[0], biases_new[1], biases_new[2], heads_new[0], heads_new[1], heads_new[2], outputs_new[0], outputs_new[1], outputs_new[2], loss_sum, weight_total)
```

```python
import functools
import math

import jax
import jax.numpy as jnp
from jax import lax
from jax.experimental import pallas as pl
from jax.experimental.pallas import tpu as pltpu
from jax.sharding import Mesh
from jax.sharding import PartitionSpec as P

DIM = 64
STEP = 10
LANES = 128
MIB = 1024 * 1024

beta_one = 0.9
beta_two = 0.999
epsilon = 1e-08
decay_rate = 0.01
table_rate = 0.2
dense_rate = 0.02

ROW = ("grp", "near")
GROUP = ("near", "col")
ALL = ("grp", "near", "col")
FAST = lax.Precision.HIGH


def adamw(weight, moment, square, gradient, rate):
    moment_next = beta_one * moment + (1.0 - beta_one) * gradient
    square_next = beta_two * square + (1.0 - beta_two) * gradient * gradient
    moment_hat = moment_next * (1.0 / (1.0 - beta_one**STEP))
    square_hat = square_next * (1.0 / (1.0 - beta_two**STEP))
    weight_next = weight - rate * (
        moment_hat / (jnp.sqrt(square_hat) + epsilon) + decay_rate * weight
    )
    return (weight_next, moment_next, square_next)


def table_adamw(weight, moment, square, gradient):
    root = math.sqrt(1.0 - beta_two**STEP)
    moment_next = beta_one * moment + (1.0 - beta_one) * gradient
    square_next = beta_two * square + (1.0 - beta_two) * (gradient * gradient)
    r = lax.rsqrt(square_next)
    below = 1.0 + (epsilon * root) * r
    near = pl.reciprocal(below, approx=True)
    near = near * (2.0 - below * near)
    ratio = (moment_next * r) * near
    weight_next = weight * (1.0 - table_rate * decay_rate) - ratio * (
        table_rate * root / (1.0 - beta_one**STEP)
    )
    return (weight_next, moment_next, square_next)


def low_half():
    return lax.broadcasted_iota(jnp.int32, (1, LANES), 1) < DIM


def gather_kernel(rows, cols, devices, each, idx_ref, table_ref, out_ref, buf, sem):
    count = devices * each

    def fetch(u):
        return pltpu.make_async_copy(
            table_ref.at[:, pl.ds(u * LANES, LANES)], buf.at[u, pl.ds(0, rows)], sem.at[u]
        )

    for u in range(cols):
        fetch(u).start()
        buf[u, pl.ds(rows, 8), :] = jnp.zeros((8, LANES), jnp.float32)
    low = low_half()
    for u in range(cols):
        fetch(u).wait()

        def step(d, carry):
            base = d * each
            for k in range(each):
                first = idx_ref[2 * u * count + base + k]
                second = idx_ref[(2 * u + 1) * count + base + k]
                out_ref[d, u, pl.ds(k, 1), :] = jnp.where(
                    low, buf[u, pl.ds(first, 1), :], buf[u, pl.ds(second, 1), :]
                )
            return carry

        lax.fori_loop(0, devices, step, 0)


def gather_rows(idx, table, devices, each):
    rows, width = table.shape
    cols = width // LANES
    return pl.pallas_call(
        functools.partial(gather_kernel, rows, cols, devices, each),
        out_shape=jax.ShapeDtypeStruct((devices, cols, each, LANES), jnp.float32),
        in_specs=[
            pl.BlockSpec(memory_space=pltpu.SMEM),
            pl.BlockSpec(memory_space=pl.ANY),
        ],
        out_specs=pl.BlockSpec(memory_space=pltpu.VMEM),
        scratch_shapes=[
            pltpu.VMEM((cols, rows + 8, LANES), jnp.float32),
            pltpu.SemaphoreType.DMA((cols,)),
        ],
        compiler_params=pltpu.CompilerParams(vmem_limit_bytes=48 * MIB),
        cost_estimate=pl.CostEstimate(
            flops=0, bytes_accessed=2 * rows * width * 4, transcendentals=0
        ),
    )(idx, table)


def pool_kernel(pieces, halves, cols, each, shift_ref, in_ref, out_ref):
    low = low_half()
    for c in range(halves):
        for u in range(cols):
            shifts = [shift_ref[c * 2 * cols + 2 * u + h] for h in range(2)]
            for a in range(pieces // 4):
                sums = []
                for s in shifts:
                    total = None
                    for j in range(4):
                        part = in_ref[lax.rem(4 * a + j + s, pieces), c, u]
                        total = part if total is None else total + part
                    sums.append(total)
                at = (c * cols + u) * LANES
                out_ref[a * each : (a + 1) * each, at : at + LANES] = jnp.where(
                    low, sums[0], sums[1]
                )


def pool(shifts, arrived):
    pieces, halves, cols, each, _ = arrived.shape
    return pl.pallas_call(
        functools.partial(pool_kernel, pieces, halves, cols, each),
        out_shape=jax.ShapeDtypeStruct(
            (pieces // 4 * each, halves * cols * LANES), jnp.float32
        ),
        in_specs=[
            pl.BlockSpec(memory_space=pltpu.SMEM),
            pl.BlockSpec(memory_space=pltpu.VMEM),
        ],
        out_specs=pl.BlockSpec(memory_space=pltpu.VMEM),
        compiler_params=pltpu.CompilerParams(vmem_limit_bytes=24 * MIB),
    )(shifts, arrived)


def spread_kernel(pieces, halves, cols, each, shift_ref, in_ref, *out_refs):
    low = low_half()
    for c in range(halves):
        for u in range(cols):
            shifts = [shift_ref[c * 2 * cols + 2 * u + h] for h in range(2)]
            at = (c * cols + u) * LANES
            for r in range(pieces):
                parts = []
                for s in shifts:
                    place = lax.rem(r - s + pieces, pieces) // 4
                    start = pl.multiple_of(place * each, each)
                    parts.append(in_ref[pl.ds(start, each), at : at + LANES])
                out_refs[u][halves * r + c] = jnp.where(low, parts[0], parts[1])


def spread(shifts, grads, pieces, halves):
    samples, width = grads.shape
    cols = width // halves // LANES
    each = samples * 4 // pieces
    return pl.pallas_call(
        functools.partial(spread_kernel, pieces, halves, cols, each),
        out_shape=[
            jax.ShapeDtypeStruct((pieces * halves, each, LANES), jnp.float32)
        ]
        * cols,
        in_specs=[
            pl.BlockSpec(memory_space=pltpu.SMEM),
            pl.BlockSpec(memory_space=pltpu.VMEM),
        ],
        out_specs=[pl.BlockSpec(memory_space=pltpu.VMEM)] * cols,
        compiler_params=pltpu.CompilerParams(vmem_limit_bytes=24 * MIB),
    )(shifts, grads)


def update_kernel(rows, part, devices, each, block, outs, idx_ref, grad_ref, *refs):
    sources, targets = refs[:3], refs[-7 - outs : -4 - outs]
    bufs, sums, in_sem, out_sem = refs[-7:-4], refs[-4:-2], refs[-2], refs[-1]
    count = devices * each
    blocks = rows // block
    columns = pl.ds(part * LANES, LANES)

    def fetch(b, k):
        at = pl.ds(b * block, block)
        return pltpu.make_async_copy(
            sources[k].at[at, columns], bufs[k].at[at], in_sem.at[k, b]
        )

    def store(b, k):
        at = pl.ds(b * block, block)
        return pltpu.make_async_copy(
            bufs[k].at[at], targets[k].at[at, columns], out_sem.at[k, b]
        )

    for b in range(blocks):
        for k in range(3):
            fetch(b, k).start()

    def clear(i, carry):
        at = pl.ds(pl.multiple_of(i * 64, 64), 64)
        for s in sums:
            s[at, :] = jnp.full((64, LANES), jnp.inf, jnp.float32)
        return carry

    lax.fori_loop(0, rows // 64, clear, 0)
    for s in sums:
        s[pl.ds(rows, 8), :] = jnp.full((8, LANES), jnp.inf, jnp.float32)

    def step(d, carry):
        for k in range(each):
            value = grad_ref[d, pl.ds(k, 1), :]
            for q in range(2):
                row = pl.ds(idx_ref[(2 * part + q) * count + d * each + k], 1)
                old = sums[q][row, :]
                sums[q][row, :] = value + jnp.where(old < jnp.inf, old, 0.0)
        return carry

    lax.fori_loop(0, devices, step, 0)

    low = low_half()
    tile = 128
    for b in range(blocks):
        for k in range(3):
            fetch(b, k).wait()

        def renew(i, carry):
            at = pl.ds(pl.multiple_of(b * block + i * tile, tile), tile)
            total = jnp.where(low, sums[0][at, :], sums[1][at, :])
            old = [buf[at, :] for buf in bufs]
            new = table_adamw(*old, total)
            hit = total < jnp.inf
            for k in range(3):
                bufs[k][at, :] = jnp.where(hit, new[k], old[k])
            return carry

        lax.fori_loop(0, block // tile, renew, 0)
        for k in range(3):
            store(b, k).start()
    for b in range(blocks):
        for k in range(3):
            store(b, k).wait()


def update_part(idx, grads, tables, part, each, previous, later):
    rows, width = tables[0].shape
    devices = grads.shape[0]
    block = rows // 8
    extra = [] if previous is None else list(previous)
    through = [] if later is None else [later]
    place = pl.BlockSpec(memory_space=pl.ANY)
    aliases = {5 + k: k for k in range(len(extra))}
    if through:
        aliases[5 + len(extra)] = 3
    done = pl.pallas_call(
        functools.partial(update_kernel, rows, part, devices, each, block, 3 + len(through)),
        out_shape=[jax.ShapeDtypeStruct((rows, width), jnp.float32)] * 3
        + [jax.ShapeDtypeStruct(x.shape, x.dtype) for x in through],
        in_specs=[
            pl.BlockSpec(memory_space=pltpu.SMEM),
            pl.BlockSpec(memory_space=pltpu.VMEM),
        ]
        + [place] * (3 + len(extra) + len(through)),
        out_specs=[place] * (3 + len(through)),
        input_output_aliases=aliases,
        scratch_shapes=[pltpu.VMEM((rows, LANES), jnp.float32)] * 3
        + [pltpu.VMEM((rows + 8, LANES), jnp.float32)] * 2
        + [pltpu.SemaphoreType.DMA((3, rows // block))] * 2,
        compiler_params=pltpu.CompilerParams(vmem_limit_bytes=48 * MIB),
        cost_estimate=pl.CostEstimate(
            flops=30 * rows * LANES, bytes_accessed=rows * LANES * 24, transcendentals=0
        ),
    )(idx, grads, *tables, *extra, *through)
    return done[:3], (done[3] if through else None)


def gelu_slope(a):
    scale = math.sqrt(2.0 / math.pi)
    t = jnp.tanh(scale * (a + 0.044715 * a * a * a))
    return 0.5 * (1.0 + t) + 0.5 * a * (1.0 - t * t) * scale * (1.0 + 3.0 * 0.044715 * a * a)


def swap_near(x):
    count = lax.axis_size("near")
    return lax.ppermute(x, "near", [(i, i ^ 1) for i in range(count)])


def swap_core(x):
    return lax.ppermute(x, "col", [(0, 1), (1, 0)])


def gather_group(x):
    pair = jnp.concatenate([x, swap_near(x)], axis=0)
    return jnp.concatenate([pair, swap_core(pair)], axis=0)


def sum_group(x):
    half = x.shape[0] // 2
    pair = x[:half] + swap_core(x[half:])
    return pair[: half // 2] + swap_near(pair[half // 2 :])


def exchange_group(x, member):
    blocks = [lax.dynamic_index_in_dim(x, member ^ i, 0, False) for i in range(4)]
    pair = jnp.stack([blocks[1], blocks[3]])
    other = swap_core(pair)
    far = swap_near(jnp.stack([blocks[2], other[1]]))
    came = jnp.stack([blocks[0], other[0], far[0], far[1]])
    return jnp.stack([lax.dynamic_index_in_dim(came, member ^ i, 0, False) for i in range(4)])


def padded(x, width):
    return jnp.pad(x, [(0, 0)] * (x.ndim - 1) + [(0, width - x.shape[-1])])


def dot(a, b, dims=((1,), (0,))):
    return lax.dot_general(
        a, b, (dims, ((), ())), precision=FAST, preferred_element_type=jnp.float32
    )


def per_device(
    tables,
    table_moment,
    table_square,
    expert_weight,
    expert_moment,
    expert_square,
    gate_weight,
    gate_moment,
    gate_square,
    tower_weight,
    tower_moment,
    tower_square,
    expert_bias,
    bias_moment,
    bias_square,
    head_bias,
    head_moment,
    head_square,
    tower_output,
    output_moment,
    output_square,
    lookup_ids,
    bag_lengths,
    sample_counts,
    labels,
    label_mask,
    sample_weight,
):
    halves = lax.axis_size("col")
    pieces = lax.axis_size("grp") * lax.axis_size("near")
    devices = pieces * halves
    groups = lax.axis_size("grp")
    members = devices // groups
    rows_here, width_here = tables.shape
    tabs_here = width_here // DIM
    samples, tabs, bag = lookup_ids.shape
    each = samples * bag // pieces
    classes = pieces // bag
    experts, depth, hidden_units = expert_weight.shape
    mine = experts // members
    tasks, tower_depth, tower_units = tower_weight.shape
    upper_width = tasks * tower_units
    member = lax.axis_index("near") * halves + lax.axis_index("col")

    def reorder(x):
        return x.reshape((each, classes) + x.shape[1:]).swapaxes(0, 1).reshape(x.shape)

    live = (jnp.arange(samples, dtype=jnp.int32) < sample_counts[0]).astype(jnp.float32)
    keep = reorder(sample_weight[:, None] * label_mask.astype(jnp.float32) * live[:, None])
    targets = reorder(labels.astype(jnp.float32))

    ids = lookup_ids.transpose(0, 2, 1).reshape(each, pieces, tabs)
    use = jnp.arange(bag, dtype=jnp.int32)[None, :, None] < bag_lengths[:, None, :]
    owner = ids // rows_here
    local = jnp.where(use.reshape(each, pieces, tabs), ids - owner * rows_here, rows_here)
    here = owner[None] == jnp.arange(pieces, dtype=jnp.int32)[:, None, None, None]
    wanted = jnp.sum(jnp.where(here, local[None], 0), axis=2)
    wanted = wanted.transpose(0, 2, 1).reshape(devices, tabs_here * each).astype(jnp.float32)
    message = jnp.concatenate(
        [wanted, jnp.broadcast_to(jnp.sum(keep), (devices, 1))], axis=1
    )
    long = -(-message.shape[1] // 1024) * 1024
    message = padded(message, long).reshape(devices, long // LANES, LANES)
    asked = lax.all_to_all(message, ALL, 0, 0, tiled=True).reshape(devices, long)
    idx = asked[:, : tabs_here * each].reshape(devices, tabs_here, each)
    idx = idx.swapaxes(0, 1).reshape(-1).astype(jnp.int32)
    weight_total = jnp.sum(asked[:, tabs_here * each])
    shifts = lookup_ids[0, :, 0] // rows_here

    lots = mine * hidden_units
    send = expert_weight.reshape(members, mine, depth, hidden_units).swapaxes(1, 2)
    send = send.reshape(members, depth, lots)
    small = jnp.concatenate(
        [
            tower_weight.swapaxes(0, 1).reshape(-1),
            gate_weight.swapaxes(0, 1).reshape(-1),
        ]
    )
    tower_flat = tower_depth * upper_width
    small_rows = -(-small.shape[0] // (8 * lots)) * 8
    small = padded(small, small_rows * lots).reshape(1, small_rows, lots)
    send = jnp.concatenate(
        [send, jnp.broadcast_to(small, (members, small_rows, lots))], axis=1
    )
    shared = exchange_group(send, member)
    shared = shared.reshape(members, depth + small_rows, lots)
    whole = lax.all_gather(shared, "grp", axis=0, tiled=True)
    weights = whole[:, :depth].reshape(devices * depth, lots)
    small = whole[:, depth:].reshape(devices, small_rows * lots)
    towers = small[:, :tower_flat].reshape(devices * tower_depth, upper_width)
    gates = small[:, tower_flat : tower_flat + depth * tasks * experts].reshape(
        devices * depth, tasks * experts
    )
    gates_mine = lax.dynamic_slice_in_dim(
        gates.reshape(devices * depth, tasks, experts), member * mine, mine, 2
    ).reshape(devices * depth, tasks * mine)
    bias_mine = lax.dynamic_slice_in_dim(expert_bias, member * mine, mine, 0).reshape(1, lots)

    picked = gather_rows(idx, tables, devices, each)
    cols = width_here // LANES
    arrived = lax.all_to_all(
        picked.reshape(devices, cols * each, LANES), ALL, 0, 0, tiled=True
    ).reshape(pieces, halves, cols, each, LANES)
    pooled = pool(shifts, arrived)
    inputs = gather_group(pooled)

    total = inputs.shape[0]
    preact = dot(inputs, weights) + bias_mine
    hidden = jax.nn.gelu(preact)
    logits = dot(inputs, gates).reshape(total, tasks, experts)
    probs = jax.nn.softmax(logits, axis=-1)
    probs_mine = lax.dynamic_slice_in_dim(probs, member * mine, mine, 2)
    parts = [
        dot(hidden[:, i * hidden_units : (i + 1) * hidden_units], towers).reshape(
            total, tasks, tower_units
        )
        for i in range(mine)
    ]
    inner_part = sum(parts[i] * probs_mine[:, :, i, None] for i in range(mine))
    mixed = sum_group(inner_part.reshape(total, upper_width)).reshape(
        samples, tasks, tower_units
    )
    inner = mixed + head_bias[None, :, :-1]
    upper = jax.nn.gelu(inner)
    score = jnp.sum(upper * tower_output[None], axis=-1) + head_bias[None, :, -1]
    loss_here = jnp.sum(keep * (jax.nn.softplus(score) - targets * score))

    d_score = keep * (jax.nn.sigmoid(score) - targets) / weight_total
    d_inner = d_score[:, :, None] * tower_output[None] * gelu_slope(inner)
    grad_output = jnp.sum(d_score[:, :, None] * upper, axis=0)
    grad_head = jnp.concatenate(
        [jnp.sum(d_inner, axis=0), jnp.sum(d_score, axis=0)[:, None]], axis=1
    )
    mean = jnp.sum(d_inner * mixed, axis=-1)
    packed = jnp.concatenate([d_inner.reshape(samples, upper_width), mean], axis=1)
    packed = padded(packed, -(-packed.shape[1] // LANES) * LANES)
    packed = gather_group(packed)
    d_inner = packed[:, :upper_width].reshape(total, tasks, tower_units)
    mean = packed[:, upper_width : upper_width + tasks]
    d_logits = []
    spreads = []
    d_hidden = []
    for i in range(mine):
        d_prob = jnp.sum(d_inner * parts[i], axis=-1)
        d_logits.append(probs_mine[:, :, i] * (d_prob - mean))
        spreads.append((d_inner * probs_mine[:, :, i, None]).reshape(total, upper_width))
        d_hidden.append(dot(spreads[i], towers, ((1,), (1,))))
    d_logits = jnp.stack(d_logits, axis=-1).reshape(total, tasks * mine)
    d_preact = jnp.concatenate(d_hidden, axis=1) * gelu_slope(preact)
    d_inputs = dot(d_preact, weights, ((1,), (1,))) + dot(d_logits, gates_mine, ((1,), (1,)))
    d_pooled = sum_group(d_inputs)

    grad_weights = dot(inputs, d_preact, ((0,), (0,)))
    grad_gates = dot(inputs, d_logits, ((0,), (0,))).reshape(devices, -1)
    grad_towers = sum(
        dot(hidden[:, i * hidden_units : (i + 1) * hidden_units], spreads[i], ((0,), (0,)))
        for i in range(mine)
    ).reshape(devices, -1)
    gate_flat = grad_gates.shape[1]
    small = padded(jnp.concatenate([grad_towers, grad_gates], axis=1), small_rows * lots)
    summed = jnp.concatenate(
        [grad_weights.reshape(devices, depth, lots), small.reshape(devices, small_rows, lots)],
        axis=1,
    )
    summed = lax.psum_scatter(summed, "grp", scatter_dimension=0, tiled=True)
    summed = exchange_group(summed, member)
    shard_experts = (
        summed[:, :depth]
        .reshape(members, depth, mine, hidden_units)
        .swapaxes(1, 2)
        .reshape(experts, depth, hidden_units)
    )
    small = summed[:, depth:].reshape(members, small_rows * lots)
    shard_towers = (
        jnp.sum(small[:, :tower_flat], axis=0)
        .reshape(tower_depth, tasks, tower_units)
        .swapaxes(0, 1)
    )
    shard_gates = (
        small[:, tower_flat : tower_flat + gate_flat]
        .reshape(members, depth, tasks, mine)
        .transpose(2, 1, 0, 3)
        .reshape(tasks, depth, experts)
    )

    grad_bias = jnp.sum(d_preact, axis=0)
    same = jnp.concatenate(
        [grad_bias, grad_head.reshape(-1), grad_output.reshape(-1), loss_here.reshape(1)]
    )
    cuts = [lots, grad_head.size, grad_output.size, 1]
    long = -(-same.shape[0] // 1024) * 1024
    same = jnp.broadcast_to(
        padded(same, long).reshape(1, long // LANES, LANES), (devices, long // LANES, LANES)
    )
    returned = list(spread(shifts, d_pooled, pieces, halves))
    returned[1] = jnp.concatenate([returned[1], same], axis=1)
    came = [lax.all_to_all(x, ALL, 0, 0, tiled=True) for x in returned[:2]]
    new_tables = None
    for u in range(cols):
        later = returned[u + 2] if u + 2 < cols else None
        new_tables, later = update_part(
            idx, came[u], (tables, table_moment, table_square), u, each, new_tables, later
        )
        if later is not None:
            came.append(lax.all_to_all(later, ALL, 0, 0, tiled=True))
    same = came[1][:, each:].reshape(devices, long)
    found = []
    start = 0
    for size in cuts:
        found.append(same[:, start : start + size])
        start += size
    summed_bias = jnp.sum(found[0].reshape(groups, members, lots), axis=0).reshape(
        experts, hidden_units
    )
    summed_head = jnp.sum(found[1], axis=0).reshape(head_bias.shape)
    summed_output = jnp.sum(found[2], axis=0).reshape(tower_output.shape)
    loss_sum = jnp.sum(found[3])

    return (
        *new_tables,
        *adamw(expert_weight, expert_moment, expert_square, shard_experts, dense_rate),
        *adamw(gate_weight, gate_moment, gate_square, shard_gates, dense_rate),
        *adamw(tower_weight, tower_moment, tower_square, shard_towers, dense_rate),
        *adamw(expert_bias, bias_moment, bias_square, summed_bias, dense_rate),
        *adamw(head_bias, head_moment, head_square, summed_head, dense_rate),
        *adamw(tower_output, output_moment, output_square, summed_output, dense_rate),
        loss_sum,
        weight_total,
    )


def solution(mesh):
    pieces, halves = mesh.devices.shape
    fine = Mesh(mesh.devices.reshape(pieces // 2, 2, halves), ALL)
    table = P(ROW, "col")
    middle = P(None, ALL, None)
    first = P(ALL)
    return jax.shard_map(
        per_device,
        mesh=fine,
        in_specs=(table,) * 3 + (middle,) * 9 + (P(),) * 9 + (first,) * 6,
        out_specs=(table,) * 3 + (middle,) * 9 + (P(),) * 11,
        check_vma=False,
    )
```

```python
import functools
import math

import jax
import jax.numpy as jnp
from jax import lax
from jax.experimental import pallas as pl
from jax.experimental.pallas import tpu as pltpu
from jax.sharding import Mesh
from jax.sharding import PartitionSpec as P

DIM = 64
STEP = 10
LANES = 128
MIB = 1024 * 1024

beta_one = 0.9
beta_two = 0.999
epsilon = 1e-08
decay_rate = 0.01
table_rate = 0.2
dense_rate = 0.02

ROW = ("hi", "near", "rest")
PEERS = ("hi", "rest")
ALL = ("hi", "near", "rest", "col")
SCALARS = pl.BlockSpec(memory_space=pltpu.SMEM)
WHOLE = pl.BlockSpec(memory_space=pltpu.VMEM)
ANYWHERE = pl.BlockSpec(memory_space=pl.ANY)


def adamw(weight, moment, square, gradient, rate):
    moment_next = beta_one * moment + (1.0 - beta_one) * gradient
    square_next = beta_two * square + (1.0 - beta_two) * gradient * gradient
    moment_hat = moment_next * (1.0 / (1.0 - beta_one**STEP))
    square_hat = square_next * (1.0 / (1.0 - beta_two**STEP))
    weight_next = weight - rate * (
        moment_hat / (jnp.sqrt(square_hat) + epsilon) + decay_rate * weight
    )
    return (weight_next, moment_next, square_next)


def table_adamw(weight, moment, square, gradient):
    root = math.sqrt(1.0 - beta_two**STEP)
    moment_next = beta_one * moment + (1.0 - beta_one) * gradient
    square_next = beta_two * square + (1.0 - beta_two) * (gradient * gradient)
    r = lax.rsqrt(square_next)
    below = 1.0 + (epsilon * root) * r
    near = pl.reciprocal(below, approx=True)
    near = near * (2.0 - below * near)
    ratio = (moment_next * r) * near
    weight_next = weight * (1.0 - table_rate * decay_rate) - ratio * (
        table_rate * root / (1.0 - beta_one**STEP)
    )
    return (weight_next, moment_next, square_next)


def fence(x, after):
    return pl.pallas_call(
        lambda *refs: None,
        out_shape=jax.ShapeDtypeStruct(x.shape, x.dtype),
        in_specs=[ANYWHERE] * (1 + len(after)),
        out_specs=ANYWHERE,
        input_output_aliases={0: 0},
        compiler_params=pltpu.CompilerParams(vmem_limit_bytes=MIB),
        cost_estimate=pl.CostEstimate(flops=0, bytes_accessed=0, transcendentals=0),
    )(x, *after)


def low_half():
    return lax.broadcasted_iota(jnp.int32, (1, LANES), 1) < DIM


def gather_kernel(rows, cols, devices, each, idx_ref, table_ref, out_ref, buf, sem):
    count = devices * each

    def fetch(u):
        return pltpu.make_async_copy(
            table_ref.at[:, pl.ds(u * LANES, LANES)], buf.at[u, pl.ds(0, rows)], sem.at[u]
        )

    for u in range(cols):
        fetch(u).start()
        buf[u, pl.ds(rows, 8), :] = jnp.zeros((8, LANES), jnp.float32)
    low = low_half()
    for u in range(cols):
        fetch(u).wait()

        def step(d, carry):
            base = d * each
            for k in range(each):
                first = idx_ref[2 * u * count + base + k]
                second = idx_ref[(2 * u + 1) * count + base + k]
                out_ref[d, u, pl.ds(k, 1), :] = jnp.where(
                    low, buf[u, pl.ds(first, 1), :], buf[u, pl.ds(second, 1), :]
                )
            return carry

        lax.fori_loop(0, devices, step, 0)


def gather_rows(idx, table, devices, each):
    rows, width = table.shape
    cols = width // LANES
    return pl.pallas_call(
        functools.partial(gather_kernel, rows, cols, devices, each),
        out_shape=jax.ShapeDtypeStruct((devices, cols, each, LANES), jnp.float32),
        in_specs=[SCALARS, ANYWHERE],
        out_specs=WHOLE,
        scratch_shapes=[
            pltpu.VMEM((cols, rows + 8, LANES), jnp.float32),
            pltpu.SemaphoreType.DMA((cols,)),
        ],
        compiler_params=pltpu.CompilerParams(vmem_limit_bytes=35 * MIB),
        cost_estimate=pl.CostEstimate(
            flops=0, bytes_accessed=2 * rows * width * 4, transcendentals=0
        ),
    )(idx, table)


def pool_kernel(pieces, halves, cols, each, place, shift_ref, peer_ref, in_ref, before, out_ref):
    low = low_half()
    stripe, spot = place
    for c in range(halves):
        for u in range(cols):
            shifts = [shift_ref[c * 2 * cols + 2 * u + h] for h in range(2)]
            bags = []
            for a in range(pieces // 4):
                sums = []
                for s in shifts:
                    total = None
                    for j in range(4):
                        part = in_ref[lax.rem(4 * a + j + s, pieces), c, u]
                        total = part if total is None else total + part
                    sums.append(total)
                bags.append(jnp.where(low, sums[0], sums[1]))
            at = (c * cols + u) * LANES
            block = jnp.concatenate(bags, axis=0).T
            for k in range(LANES // stripe):
                to = pl.multiple_of(spot(at // stripe + k, peer_ref[0]) * stripe, stripe)
                out_ref[pl.ds(to, stripe), :] = block[k * stripe : (k + 1) * stripe]


def pool(shifts, peer, place, arrived, before):
    pieces, halves, cols, each, _ = arrived.shape
    return pl.pallas_call(
        functools.partial(pool_kernel, pieces, halves, cols, each, place),
        out_shape=jax.ShapeDtypeStruct(
            (halves * cols * LANES, pieces // 4 * each), jnp.float32
        ),
        in_specs=[SCALARS, SCALARS, WHOLE, ANYWHERE],
        out_specs=WHOLE,
        compiler_params=pltpu.CompilerParams(vmem_limit_bytes=8 * MIB),
    )(shifts, peer, arrived, before)


def spread_kernel(terms, pieces, halves, cols, each, place, shift_ref, peer_ref, *refs):
    low = low_half()
    stripe, spot = place
    in_refs, out_refs, rows = refs[:terms], refs[terms:-1], refs[-1]
    for c in range(halves):
        for u in range(cols):
            shifts = [shift_ref[c * 2 * cols + 2 * u + h] for h in range(2)]
            at = (c * cols + u) * LANES
            block = []
            for k in range(LANES // stripe):
                where = pl.multiple_of(spot(at // stripe + k, peer_ref[0]) * stripe, stripe)
                block.append(sum(ref[pl.ds(where, stripe), :] for ref in in_refs))
            rows[c * cols + u] = jnp.concatenate(block, axis=0).T
            for r in range(pieces):
                parts = []
                for s in shifts:
                    place = lax.rem(r - s + pieces, pieces) // 4
                    start = pl.multiple_of(place * each, each)
                    parts.append(rows[c * cols + u, pl.ds(start, each), :])
                out_refs[u][halves * r + c] = jnp.where(low, parts[0], parts[1])


def spread(shifts, peer, place, terms, pieces, halves):
    width, samples = terms[0].shape
    cols = width // halves // LANES
    each = samples * 4 // pieces
    return pl.pallas_call(
        functools.partial(spread_kernel, len(terms), pieces, halves, cols, each, place),
        out_shape=[
            jax.ShapeDtypeStruct((pieces * halves, each, LANES), jnp.float32)
        ]
        * cols,
        in_specs=[SCALARS, SCALARS] + [WHOLE] * len(terms),
        out_specs=[WHOLE] * cols,
        scratch_shapes=[pltpu.VMEM((width // LANES, samples, LANES), jnp.float32)],
        compiler_params=pltpu.CompilerParams(vmem_limit_bytes=10 * MIB),
    )(shifts, peer, *terms)


def update_kernel(rows, part, devices, each, block, outs, idx_ref, grad_ref, *refs):
    sources, targets = refs[:3], refs[-7 - outs : -4 - outs]
    bufs, sums, in_sem, out_sem = refs[-7:-4], refs[-4:-2], refs[-2], refs[-1]
    count = devices * each
    blocks = rows // block
    columns = pl.ds(part * LANES, LANES)

    def fetch(b, k):
        at = pl.ds(b * block, block)
        return pltpu.make_async_copy(
            sources[k].at[at, columns], bufs[k].at[at], in_sem.at[k, b]
        )

    def store(b, k):
        at = pl.ds(b * block, block)
        return pltpu.make_async_copy(
            bufs[k].at[at], targets[k].at[at, columns], out_sem.at[k, b]
        )

    for b in range(blocks):
        for k in range(3):
            fetch(b, k).start()

    def clear(i, carry):
        at = pl.ds(pl.multiple_of(i * 64, 64), 64)
        for s in sums:
            s[at, :] = jnp.full((64, LANES), jnp.inf, jnp.float32)
        return carry

    lax.fori_loop(0, rows // 64, clear, 0)
    for s in sums:
        s[pl.ds(rows, 8), :] = jnp.full((8, LANES), jnp.inf, jnp.float32)

    def step(d, carry):
        for k in range(each):
            value = grad_ref[d, pl.ds(k, 1), :]
            for q in range(2):
                row = pl.ds(idx_ref[(2 * part + q) * count + d * each + k], 1)
                old = sums[q][row, :]
                sums[q][row, :] = value + jnp.where(old < jnp.inf, old, 0.0)
        return carry

    lax.fori_loop(0, devices, step, 0)

    low = low_half()
    tile = 128
    for b in range(blocks):
        for k in range(3):
            fetch(b, k).wait()

        def renew(i, carry):
            at = pl.ds(pl.multiple_of(b * block + i * tile, tile), tile)
            total = jnp.where(low, sums[0][at, :], sums[1][at, :])
            old = [buf[at, :] for buf in bufs]
            new = table_adamw(*old, total)
            hit = total < jnp.inf
            for k in range(3):
                bufs[k][at, :] = jnp.where(hit, new[k], old[k])
            return carry

        lax.fori_loop(0, block // tile, renew, 0)
        for k in range(3):
            store(b, k).start()
    for b in range(blocks):
        for k in range(3):
            store(b, k).wait()


def update_part(idx, grads, tables, part, each, previous, through, before):
    rows, width = tables[0].shape
    devices = grads.shape[0]
    block = rows // 8
    extra = [] if previous is None else list(previous)
    place = pl.BlockSpec(memory_space=pl.ANY)
    handed = extra + list(through)
    first = 0 if extra else 3
    outs = 3 + len(through)
    done = pl.pallas_call(
        functools.partial(update_kernel, rows, part, devices, each, block, outs),
        out_shape=[jax.ShapeDtypeStruct((rows, width), jnp.float32)] * 3
        + [jax.ShapeDtypeStruct(x.shape, x.dtype) for x in through],
        in_specs=[SCALARS, WHOLE] + [place] * (3 + len(handed) + len(before)),
        out_specs=[place] * outs,
        input_output_aliases={5 + k: first + k for k in range(len(handed))},
        scratch_shapes=[pltpu.VMEM((rows, LANES), jnp.float32)] * 3
        + [pltpu.VMEM((rows + 8, LANES), jnp.float32)] * 2
        + [pltpu.SemaphoreType.DMA((3, rows // block))] * 2,
        compiler_params=pltpu.CompilerParams(vmem_limit_bytes=42 * MIB),
        cost_estimate=pl.CostEstimate(
            flops=30 * rows * LANES, bytes_accessed=rows * LANES * 24, transcendentals=0
        ),
    )(idx, grads, *tables, *handed, *before)
    return done[:3], list(done[3:])


GELU_SCALE = math.sqrt(2.0 / math.pi)


def gelu(a):
    return 0.5 * a * (1.0 + jnp.tanh(GELU_SCALE * (a + 0.044715 * (a * a * a))))


def gelu_slope(a):
    square = a * a
    t = jnp.tanh(GELU_SCALE * a * (1.0 + 0.044715 * square))
    return 0.5 * (1.0 + t) + (0.5 * GELU_SCALE) * a * (1.0 - t * t) * (
        1.0 + (3.0 * 0.044715) * square
    )


def split(x):
    high = x.astype(jnp.bfloat16)
    return high, (x - high.astype(jnp.float32)).astype(jnp.bfloat16)


def product(a, b, flip=False):
    dims = (((1,), (1 if flip else 0,)), ((), ()))

    def one(x, y):
        return lax.dot_general(x, y, dims, preferred_element_type=jnp.float32)

    return one(a[0], b[0]) + (one(a[0], b[1]) + one(a[1], b[0]))


TOWER_LANES = 384
GATE_LANES = 64


def pack_rows(tower, gate, width):
    def eights(x, lanes):
        x = jnp.pad(x, ((0, -x.shape[0] % 8), (0, lanes - x.shape[1])))
        return x.reshape(-1, 8, lanes).swapaxes(0, 1).reshape(8, -1)

    return padded(
        jnp.concatenate([eights(tower, TOWER_LANES), eights(gate, GATE_LANES)], axis=1), width
    )


def unpack_rows(x, tower_shape, gate_shape):
    def rows(x, shape, lanes):
        x = x.reshape(8, -1, lanes).swapaxes(0, 1).reshape(-1, lanes)
        return x[: shape[0], : shape[1]]

    cut = -(-tower_shape[0] // 8) * TOWER_LANES
    end = cut + gate_shape[0] // 8 * GATE_LANES
    return rows(x[:, :cut], tower_shape, TOWER_LANES), rows(x[:, cut:end], gate_shape, GATE_LANES)


def tower_row(order, peer_ref, number, member, tower_depth):
    rest, counted = order
    place = number ^ peer_ref[0] if counted else number
    device = ((place // rest * 2 + member // 2) * rest + place % rest) * 2 + member % 2
    row = device * tower_depth
    return pl.multiple_of(row, tower_depth) if counted else row


def split_kernel(depth, tower_depth, order, pieces, peer_ref, *refs):
    outs = refs[pieces : -3 - pieces]
    piece_refs, (tower, gate, sem) = refs[-3 - pieces : -3], refs[-3:]
    loads = [
        pltpu.make_async_copy(refs[k], piece_refs[k], sem.at[k]) for k in range(pieces)
    ]
    for load in loads:
        load.start()

    def put(k, at, value):
        high, low = split(value)
        outs[k][at] = high
        outs[k + 1][at] = low

    block = 0
    gate_at = -(-tower_depth // 8) * TOWER_LANES
    gate[...] = jnp.zeros(gate.shape, jnp.float32)
    for load, ref in zip(loads, piece_refs):
        load.wait()
        step = min(LANES // depth, ref.shape[0])
        for b in range(0, ref.shape[0], step):
            rows = slice((block + b) * depth, (block + b + step) * depth)
            put(0, (rows, slice(None)), ref[b : b + step, :depth, :].reshape(-1, ref.shape[2]))
        for b in range(ref.shape[0]):
            number, member = (block + b) // 4, (block + b) % 4
            row = tower_row(order, peer_ref, number, member, tower_depth)
            for k in range(0, tower_depth, 8):
                high = min(8, tower_depth)
                at = k // 8 * TOWER_LANES
                tower[pl.ds(row + k, high), :] = ref[
                    b, depth : depth + high, at : at + TOWER_LANES
                ]
            for k in range(0, depth, LANES // GATE_LANES * 8):
                at = gate_at + k // 8 * GATE_LANES
                both = ref[b, depth : depth + 8, at : at + LANES]
                row = (block + b) * depth + k
                gate[row : row + 8, :GATE_LANES] = both[:, :GATE_LANES]
                if k + 8 < depth:
                    gate[row + 8 : row + 16, :GATE_LANES] = both[:, GATE_LANES:]
        block += ref.shape[0]
    for b in range(outs[0].shape[0] // LANES):
        rows = slice(b * LANES, (b + 1) * LANES)
        for k in range(2):
            turned = outs[k][rows, :].astype(jnp.float32).T
            outs[2 + k][:, rows] = turned.astype(jnp.bfloat16)
    width = outs[4].shape[1]
    put(4, Ellipsis, tower[:, :width])
    put(6, Ellipsis, gate[:, :GATE_LANES])
    put(8, Ellipsis, tower[...].T[:width])
    put(10, Ellipsis, gate[...].T[:GATE_LANES])


def split_weights(pieces, peer, order, depth, tower_depth, tower_width):
    lots = pieces[0].shape[2]
    devices = sum(x.shape[0] for x in pieces)
    width = devices * depth
    height = devices * tower_depth
    shapes = [(width, lots), (lots, width), (height, tower_width), (width, GATE_LANES)]
    shapes += [shapes[2][::-1], shapes[3][::-1]]
    return pl.pallas_call(
        functools.partial(split_kernel, depth, tower_depth, order, len(pieces)),
        out_shape=[
            jax.ShapeDtypeStruct(shape, jnp.bfloat16) for shape in shapes for _ in range(2)
        ],
        in_specs=[SCALARS] + [ANYWHERE] * len(pieces),
        out_specs=[WHOLE] * 12,
        scratch_shapes=[pltpu.VMEM(x.shape, x.dtype) for x in pieces]
        + [
            pltpu.VMEM((height, TOWER_LANES), jnp.float32),
            pltpu.VMEM((width, LANES), jnp.float32),
            pltpu.SemaphoreType.DMA((len(pieces),)),
        ],
        compiler_params=pltpu.CompilerParams(vmem_limit_bytes=16 * MIB),
    )(peer, *pieces)


def forward_kernel(dims, member_ref, *refs):
    tasks, experts, mine, hidden_units, tower_units = dims
    x_refs, refs = refs[:2], refs[2:]
    weight, tower, gate = [(refs[2 * k], refs[2 * k + 1]) for k in range(3)]
    bias_ref, pre_ref, prob_ref, upper_ref, part_ref, x_high, x_low, hid_ref = refs[6:]
    for k in range(2):
        at = slice(k * LANES, (k + 1) * LANES)
        x_high[:, at], x_low[:, at] = split(x_refs[k][...])
    lots = pre_ref.shape[0]
    tile = 256

    def rows(i, carry):
        at = pl.ds(pl.multiple_of(i * tile, tile), tile)
        pre = product([w[at, :] for w in weight], [x_high[...], x_low[...]]) + bias_ref[at, :]
        pre_ref[at, :] = pre
        hid_ref[at, :] = gelu(pre)
        return carry

    lax.fori_loop(0, lots // tile, rows, 0)
    logits = product([g[...] for g in gate], [x_high[...], x_low[...]])
    total = logits.shape[1]
    logits = logits[: tasks * experts].reshape(tasks, experts, total)
    grown = jnp.exp(logits - jnp.max(logits, axis=1, keepdims=True))
    probs = grown / jnp.sum(grown, axis=1, keepdims=True)
    prob_ref[...] = probs.reshape(tasks * experts, total)
    which = lax.broadcasted_iota(jnp.int32, probs.shape, 1)
    part = jnp.zeros((tasks, tower_units, total), jnp.float32)
    for i in range(mine):
        own = jnp.sum(
            jnp.where(which == member_ref[0] * mine + i, probs, 0.0), axis=1, keepdims=True
        )
        hidden = hid_ref[i * hidden_units : (i + 1) * hidden_units, :]
        upper = product([t[...] for t in tower], split(hidden))
        upper_ref[i] = upper
        part = part + own * upper.reshape(tasks, tower_units, total)
    part = part.reshape(tasks * tower_units, total)
    part_ref[0] = part[:, :LANES]
    part_ref[1] = part[:, LANES:]


def forward(dims, member, xs, weight, tower, gate, bias):
    tasks, experts, mine, hidden_units, tower_units = dims
    lots = mine * hidden_units
    width = tasks * tower_units
    total = 2 * LANES
    shapes = [
        (lots, total),
        (tasks * experts, total),
        (mine, width, total),
        (2, width, LANES),
    ]
    return pl.pallas_call(
        functools.partial(forward_kernel, dims),
        out_shape=[jax.ShapeDtypeStruct(shape, jnp.float32) for shape in shapes],
        in_specs=[SCALARS] + [WHOLE] * 9,
        out_specs=[WHOLE] * 4,
        scratch_shapes=[pltpu.VMEM((xs[0].shape[0], total), jnp.bfloat16)] * 2
        + [pltpu.VMEM((lots, total), jnp.float32)],
        compiler_params=pltpu.CompilerParams(vmem_limit_bytes=16 * MIB),
        cost_estimate=pl.CostEstimate(
            flops=8 * lots * xs[0].shape[0] * total,
            bytes_accessed=12 * MIB,
            transcendentals=lots * total,
        ),
    )(member, *xs, *weight, *tower, *gate, bias)


def score_kernel(
    tasks, total_ref, first_ref, second_ref, bias_ref, out_ref, last_ref, keep_ref, target_ref,
    packed_ref, grad_out_ref, grad_bias_ref, small_ref,
):
    mixed = first_ref[...] + second_ref[...]
    width, samples = mixed.shape

    def by_task(x):
        return x.reshape(tasks, width // tasks, samples)

    inner = mixed + bias_ref[...]
    upper = gelu(inner)
    keep = keep_ref[...]
    targets = target_ref[...]
    score = jnp.sum(by_task(upper * out_ref[...]), axis=1) + last_ref[...]
    faded = jnp.exp(-jnp.abs(score))
    softplus = jnp.maximum(score, 0.0) + jnp.log1p(faded)
    sigmoid = jnp.where(score >= 0.0, 1.0, faded) / (1.0 + faded)
    d_score = keep * (sigmoid - targets) / total_ref[0]
    wide = jnp.broadcast_to(d_score[:, None, :], by_task(mixed).shape).reshape(width, samples)
    d_inner = wide * out_ref[...] * gelu_slope(inner)
    packed_ref[:width, :] = d_inner
    mean = jnp.sum(by_task(d_inner * mixed), axis=1)
    packed_ref[width:, :] = jnp.concatenate(
        [mean, jnp.zeros((packed_ref.shape[0] - width - tasks, samples), jnp.float32)], axis=0
    )
    grad_out_ref[...] = jnp.sum(wide * upper, axis=1, keepdims=True)
    grad_bias_ref[...] = jnp.sum(d_inner, axis=1, keepdims=True)
    small_ref[0] = jnp.sum(d_score, axis=1, keepdims=True)
    small_ref[1] = jnp.sum(keep * (softplus - targets * score), axis=1, keepdims=True)


def score_step(tasks, weight_total, first, second, bias, out, last, keep, targets):
    width, samples = first.shape
    shapes = [(-(-(width + tasks) // 8) * 8, samples), (width, 1), (width, 1), (2, tasks, 1)]
    return pl.pallas_call(
        functools.partial(score_kernel, tasks),
        out_shape=[jax.ShapeDtypeStruct(shape, jnp.float32) for shape in shapes],
        in_specs=[SCALARS] + [WHOLE] * 7,
        out_specs=[WHOLE] * 4,
        compiler_params=pltpu.CompilerParams(vmem_limit_bytes=8 * MIB),
    )(weight_total, first, second, bias, out, last, keep, targets)


def backward_kernel(dims, member_ref, *refs):
    tasks, experts, mine, hidden_units, tower_units = dims
    width = tasks * tower_units
    packed_refs, refs = refs[:2], refs[2:]
    pre_ref, prob_ref, upper_ref = refs[:3]
    weight, tower, gate = [(refs[3 + 2 * k], refs[4 + 2 * k]) for k in range(3)]
    d_pre_ref, spread_ref, logit_ref, near_ref, far_ref, high_ref, low_ref = refs[9:]
    total = 2 * LANES
    packed = jnp.concatenate([ref[...] for ref in packed_refs], axis=1)
    d_inner = packed[:width].reshape(tasks, tower_units, total)
    mean = packed[width : width + 8].reshape(1, 8, total)[0][:tasks]
    probs = prob_ref[...].reshape(tasks, experts, total)
    which = lax.broadcasted_iota(jnp.int32, probs.shape, 1)
    d_logits = jnp.zeros(probs.shape, jnp.float32)
    for i in range(mine):
        chosen = which == member_ref[0] * mine + i
        own = jnp.sum(jnp.where(chosen, probs, 0.0), axis=1, keepdims=True)
        d_prob = jnp.sum(d_inner * upper_ref[i].reshape(d_inner.shape), axis=1)
        d_logit = own * (d_prob - mean)[:, None, :]
        d_logits = jnp.where(chosen, d_logit, d_logits)
        spreads = (d_inner * own).reshape(width, total)
        spread_ref[i] = spreads
        at = slice(i * hidden_units, (i + 1) * hidden_units)
        d_hidden = product([t[...] for t in tower], split(spreads))
        d_pre = d_hidden * gelu_slope(pre_ref[at, :])
        d_pre_ref[at, :] = d_pre
        high_ref[at, :], low_ref[at, :] = split(d_pre)
    d_logits = d_logits.reshape(tasks * experts, total)
    d_logits = jnp.concatenate(
        [d_logits, jnp.zeros((GATE_LANES - tasks * experts, total), jnp.float32)], axis=0
    )
    logit_ref[...] = d_logits
    d_logits = split(d_logits)
    tile = 256

    def rows(i, carry):
        at = pl.ds(pl.multiple_of(i * tile, tile), tile)
        value = product([w[at, :] for w in weight], [high_ref[...], low_ref[...]])
        value = value + product([g[at, :] for g in gate], d_logits)
        near_ref[at, :] = value[:, :LANES]
        far_ref[at, :] = value[:, LANES:]
        return carry

    lax.fori_loop(0, near_ref.shape[0] // tile, rows, 0)


def backward(dims, member, packed, pre, probs, upper, weight, tower, gate):
    tasks, experts, mine, hidden_units, tower_units = dims
    lots = mine * hidden_units
    depth = weight[0].shape[0]
    total = 2 * LANES
    shapes = [
        (lots, total),
        (mine, tasks * tower_units, total),
        (GATE_LANES, total),
        (depth, LANES),
        (depth, LANES),
    ]
    return pl.pallas_call(
        functools.partial(backward_kernel, dims),
        out_shape=[jax.ShapeDtypeStruct(shape, jnp.float32) for shape in shapes],
        in_specs=[SCALARS] + [WHOLE] * 11,
        out_specs=[WHOLE] * 5,
        scratch_shapes=[pltpu.VMEM((lots, total), jnp.bfloat16)] * 2,
        compiler_params=pltpu.CompilerParams(vmem_limit_bytes=16 * MIB),
        cost_estimate=pl.CostEstimate(
            flops=8 * lots * depth * total, bytes_accessed=12 * MIB, transcendentals=lots * total
        ),
    )(member, *packed, pre, probs, upper, *weight, *tower, *gate)


def gradient_kernel(dims, depth, tower_depth, order, outs, peer_ref, *refs):
    mine, hidden_units = dims
    logits, sources, refs = refs[:2], refs[2:12], refs[13:]
    weight_refs, bias_ref, refs = refs[:outs], refs[outs], refs[outs + 1 :]
    held, (x_high, x_low, d_high, d_low, tower, in_sem) = refs[:10], refs[10:]
    loads = [pltpu.make_async_copy(sources[k], held[k], in_sem.at[k]) for k in range(10)]
    for load in loads:
        load.start()
    lots = d_high.shape[0]
    tile = LANES
    share = tile // depth
    tiles = x_high.shape[0] // tile
    gate_at = -(-tower_depth // 8) * TOWER_LANES
    gate_end = gate_at + depth // 8 * GATE_LANES
    for k in range(4):
        at = slice(k * LANES, (k + 1) * LANES)
        loads[k].wait()
        x_high[:, at], x_low[:, at] = split(held[k][...])
    bias = None
    for k in range(2):
        at = slice(2 * k * LANES, 2 * (k + 1) * LANES)
        loads[4 + k].wait()
        value = held[4 + k][...]
        d_high[:, at], d_low[:, at] = split(value)
        part = jnp.sum(value, axis=1, keepdims=True)
        bias = part if bias is None else bias + part
    bias_ref[...] = bias
    for k in range(6, 10):
        loads[k].wait()

    def parts(i):
        if outs == 1:
            return [(weight_refs[0], (), i * share, share)]
        high, middle, low = i // 4, i // 2 % 2, i % 2
        return [(weight_refs[low], (high, middle), 0, 2), (weight_refs[2 + middle], (high, low), 0, 2)]

    wide = 256

    def columns(n, carry):
        at = pl.ds(pl.multiple_of(n * wide, wide), wide)
        value = product([x_high[...], x_low[...]], [d_high[at, :], d_low[at, :]], True)
        for i in range(tiles):
            row = i * tile
            for ref, where, first, many in parts(i):
                ref[(*where, slice(first, first + many), slice(0, depth), at)] = value[
                    row : row + many * depth
                ].reshape(many, depth, wide)
                row += many * depth
        return carry

    lax.fori_loop(0, lots // wide, columns, 0)
    d_logits = split(jnp.concatenate([ref[...] for ref in logits], axis=1))
    gates = product([x_high[...], x_low[...]], d_logits, True)
    value = None
    for i in range(mine):
        for k in range(2):
            hidden = gelu(held[6 + k][i * hidden_units : (i + 1) * hidden_units, :])
            part = product(split(hidden), split(held[8 + k][i]), True)
            value = part if value is None else value + part
    tower[...] = jnp.concatenate(
        [value, jnp.zeros((value.shape[0], TOWER_LANES - value.shape[1]), jnp.float32)], axis=1
    )
    full = gate_end == lots and tower_depth % 8 == 0
    for i in range(tiles):
        d = i * share
        for ref, where, first, many in parts(i):
            for k in range(first, first + many):
                if not full:
                    ref[(*where, k, slice(depth, depth + 8), slice(None))] = jnp.zeros(
                        (8, lots), jnp.float32
                    )
                row = tower_row(order, peer_ref, d // 4, d % 4, tower_depth)
                for j in range(0, tower_depth, 8):
                    high = min(8, tower_depth)
                    to = j // 8 * TOWER_LANES
                    ref[(*where, k, slice(depth, depth + high), slice(to, to + TOWER_LANES))] = (
                        tower[pl.ds(row + j, high), :]
                    )
                eights = [gates[d * depth + j : d * depth + j + 8] for j in range(0, depth, 8)]
                ref[(*where, k, slice(depth, depth + 8), slice(gate_at, gate_end))] = (
                    jnp.concatenate(eights, axis=1) if len(eights) > 1 else eights[0]
                )
                d += 1


def gradients(dims, devices, depth, tower_depth, order, peer, logits, operands, before):
    mine, hidden_units = dims
    lots = mine * hidden_units
    tall = depth + 8
    counted = order[1]
    shape = (2, 2, 2, tall, lots) if counted else (devices, tall, lots)
    outs = 4 if counted else 1
    return pl.pallas_call(
        functools.partial(gradient_kernel, dims, depth, tower_depth, order, outs),
        out_shape=[jax.ShapeDtypeStruct(shape, jnp.float32)] * outs
        + [jax.ShapeDtypeStruct((lots, 1), jnp.float32)],
        in_specs=[SCALARS, WHOLE, WHOLE] + [ANYWHERE] * 11,
        out_specs=[WHOLE] * (outs + 1),
        scratch_shapes=[pltpu.VMEM(x.shape, x.dtype) for x in operands]
        + [pltpu.VMEM((devices * depth, 4 * LANES), jnp.bfloat16)] * 2
        + [pltpu.VMEM((lots, 4 * LANES), jnp.bfloat16)] * 2
        + [
            pltpu.VMEM((hidden_units, TOWER_LANES), jnp.float32),
            pltpu.SemaphoreType.DMA((10,)),
        ],
        compiler_params=pltpu.CompilerParams(vmem_limit_bytes=28 * MIB),
        cost_estimate=pl.CostEstimate(
            flops=16 * lots * devices * depth * LANES,
            bytes_accessed=16 * MIB,
            transcendentals=0,
        ),
    )(peer, *logits, *operands, before)


def swap_near(x):
    count = lax.axis_size("near")
    return lax.ppermute(x, "near", [(i, i ^ 1) for i in range(count)])


def swap_core(x):
    return lax.ppermute(x, "col", [(0, 1), (1, 0)])


def exchange_cores(x, member):
    blocks = [lax.dynamic_index_in_dim(x, member ^ i, 0, False) for i in range(4)]
    return blocks, swap_core(jnp.stack([blocks[1], blocks[3]]))


def exchange_chips(state, member, after=0):
    blocks, other = state
    far = swap_near(jnp.stack([blocks[2], other[1]]))
    came = jnp.stack([blocks[0], other[0], far[0], far[1]])
    member = member + after
    return jnp.stack([lax.dynamic_index_in_dim(came, member ^ i, 0, False) for i in range(4)])


def swap_peer(x, bit):
    if bit == 4:
        return lax.ppermute(x, "hi", [(0, 1), (1, 0)])
    return lax.ppermute(x, "rest", [(i, i ^ bit) for i in range(lax.axis_size("rest"))])


def near_peers(x):
    return [swap_peer(x, bit) for bit in (1, 2, 4)]


def gather_peers(x, one, two, top):
    cut = x.shape[0] // 2

    def plane(own, one, two):
        far = [swap_peer(two[:cut], 1), swap_peer(one[cut:], 2)]
        return [own, one, two] + far

    return plane(x, one, two) + plane(top, swap_peer(top, 1), swap_peer(top, 2))


def both_sums(x, far, axis):
    return [
        lax.index_in_dim(x, i, axis, False) + lax.index_in_dim(far, i, axis, False)
        for i in range(2)
    ]


def padded(x, width):
    return jnp.pad(x, [(0, 0)] * (x.ndim - 1) + [(0, width - x.shape[-1])])


def per_device(
    tables,
    table_moment,
    table_square,
    expert_weight,
    expert_moment,
    expert_square,
    gate_weight,
    gate_moment,
    gate_square,
    tower_weight,
    tower_moment,
    tower_square,
    expert_bias,
    bias_moment,
    bias_square,
    head_bias,
    head_moment,
    head_square,
    tower_output,
    output_moment,
    output_square,
    lookup_ids,
    bag_lengths,
    sample_counts,
    labels,
    label_mask,
    sample_weight,
):
    halves = lax.axis_size("col")
    rest = lax.axis_size("rest")
    pieces = 4 * rest
    devices = pieces * halves
    groups = 2 * rest
    members = devices // groups
    rows_here, width_here = tables.shape
    tabs_here = width_here // DIM
    samples, tabs, bag = lookup_ids.shape
    each = samples * bag // pieces
    classes = pieces // bag
    experts, depth, hidden_units = expert_weight.shape
    mine = experts // members
    tasks, tower_depth, tower_units = tower_weight.shape
    upper_width = tasks * tower_units
    member = lax.axis_index("near") * halves + lax.axis_index("col")
    counted = groups == 8
    peer = lax.axis_index("hi") * rest + lax.axis_index("rest") if counted else jnp.int32(0)
    peer_at = peer.astype(jnp.int32).reshape(1)
    depth = expert_weight.shape[1]

    def spot(stripe, own):
        high, near, low = stripe // (2 * rest), stripe // rest % 2, stripe % rest
        return ((high * rest + low) ^ own) * 2 + near

    place = (halves * depth, spot)

    order = (rest, counted)

    def reorder(x):
        return x.reshape((each, classes) + x.shape[1:]).swapaxes(0, 1).reshape(x.shape)

    live = (jnp.arange(samples, dtype=jnp.int32) < sample_counts[0]).astype(jnp.float32)
    keep = reorder(sample_weight[:, None] * label_mask.astype(jnp.float32) * live[:, None])
    targets = reorder(labels.astype(jnp.float32))

    ids = lookup_ids.transpose(0, 2, 1).reshape(each, pieces, tabs)
    use = jnp.arange(bag, dtype=jnp.int32)[None, :, None] < bag_lengths[:, None, :]
    owner = ids // rows_here
    local = jnp.where(use.reshape(each, pieces, tabs), ids - owner * rows_here, rows_here)
    here = owner[None] == jnp.arange(pieces, dtype=jnp.int32)[:, None, None, None]
    wanted = jnp.sum(jnp.where(here, local[None], 0), axis=2)
    wanted = wanted.transpose(0, 2, 1).reshape(devices, tabs_here * each).astype(jnp.float32)
    message = jnp.concatenate(
        [wanted, jnp.broadcast_to(jnp.sum(keep), (devices, 1))], axis=1
    )
    wide = -(-message.shape[1] // 1024) * 1024
    message = padded(message, wide).reshape(devices, wide // LANES, LANES)
    shifts = lookup_ids[0, :, 0] // rows_here

    asked = lax.all_to_all(message, ALL, 0, 0, tiled=True).reshape(devices, wide)
    idx = asked[:, : tabs_here * each].reshape(devices, tabs_here, each)
    idx = idx.swapaxes(0, 1).reshape(-1).astype(jnp.int32)
    weight_total = jnp.sum(asked[:, tabs_here * each])

    lots = mine * hidden_units
    send = expert_weight.reshape(members, mine, depth, hidden_units).swapaxes(1, 2)
    send = send.reshape(members, depth, lots)
    small = pack_rows(
        tower_weight.swapaxes(0, 1).reshape(tower_depth, upper_width),
        gate_weight.swapaxes(0, 1).reshape(depth, tasks * experts),
        lots,
    )
    send = jnp.concatenate(
        [send, jnp.broadcast_to(small[None], (members,) + small.shape)], axis=1
    )
    ready = jnp.minimum(idx[0], 0)
    shared = exchange_chips(exchange_cores(send, member), member, ready)
    if counted:
        round_one = near_peers(shared)
        parts = gather_peers(shared, *round_one)
    else:
        round_one = [shared]
        parts = [lax.all_gather(shared, PEERS, axis=0, tiled=True)]
    bias_mine = lax.dynamic_slice_in_dim(expert_bias, member * mine, mine, 0).reshape(lots, 1)

    picked = fence(gather_rows(idx, tables, devices, each), round_one)
    cols = width_here // LANES
    arrived = lax.all_to_all(
        picked.reshape(devices, cols * each, LANES), ALL, 0, 0, tiled=True
    ).reshape(pieces, halves, cols, each, LANES)
    split_parts = split_weights(
        parts, peer_at, order, depth, tower_depth, upper_width
    )
    weight_pair, weight_turned, tower_pair, gate_pair, tower_turned, gate_turned = [
        split_parts[2 * k : 2 * k + 2] for k in range(6)
    ]
    mine_x = pool(shifts, peer_at, place, arrived, split_parts[0])
    near_x = swap_near(mine_x)
    halves_x = [(mine_x, swap_core(mine_x)), (near_x, swap_core(near_x))]

    dims = (tasks, experts, mine, hidden_units, tower_units)
    member_at = member.astype(jnp.int32).reshape(1)
    runs = [
        forward(dims, member_at, x, weight_turned, tower_turned, gate_turned, bias_mine)
        for x in halves_x
    ]
    part_own, part_near = runs[0][3], runs[1][3]
    first = part_own[0] + swap_core(part_own[1])
    second = swap_near(part_near[0] + swap_core(part_near[1]))
    packed, grad_output, grad_head, few = score_step(
        tasks,
        weight_total.reshape(1),
        first,
        second,
        head_bias[:, :-1].reshape(upper_width, 1),
        tower_output.reshape(upper_width, 1),
        head_bias[:, -1:],
        keep.T,
        targets.T,
    )

    near_packed = swap_near(packed)
    halves_packed = [(packed, swap_core(packed)), (near_packed, swap_core(near_packed))]

    def half_back(k, packed):
        run = runs[k]
        return backward(
            dims,
            member_at,
            packed,
            run[0],
            run[1],
            run[2],
            weight_pair,
            tower_pair,
            gate_pair,
        )

    back_near = half_back(1, halves_packed[1])
    (near_in, far_in) = back_near[3:]
    leaving = near_in + swap_core(far_in)
    beyond = swap_near(leaving)
    back = [half_back(0, (fence(packed, [leaving]), halves_packed[0][1])), back_near]
    d_terms = [back[0][3], swap_core(back[0][4]), beyond]

    returned = list(spread(shifts, peer_at, place, d_terms, pieces, halves))

    *sums, grad_bias = gradients(
        (mine, hidden_units),
        devices,
        depth,
        tower_depth,
        order,
        peer_at,
        [x[2] for x in back],
        [
            *halves_x[0],
            *halves_x[1],
            *[x[0] for x in back],
            *[x[0] for x in runs],
            *[x[1] for x in back],
        ],
        returned[0],
    )

    grad_head = jnp.concatenate([grad_head.reshape(tasks, tower_units), few[0]], axis=1)
    same = jnp.concatenate(
        [
            grad_bias.reshape(-1),
            grad_head.reshape(-1),
            grad_output.reshape(-1),
            jnp.sum(few[1]).reshape(1),
        ]
    )
    cuts = [lots, grad_head.size, grad_output.size, 1]
    long = -(-same.shape[0] // 1024) * 1024
    same = jnp.broadcast_to(
        padded(same, long).reshape(1, long // LANES, LANES), (devices, long // LANES, LANES)
    )
    returned[1] = jnp.concatenate([returned[1], same], axis=1)
    came = [lax.all_to_all(x, ALL, 0, 0, tiled=True) for x in returned[:2]]
    new_tables = None
    before = []
    if counted:
        kept = [sums[0], sums[2]]
        far = [swap_peer(sums[1], 1), swap_peer(sums[3], 2)]
    else:
        kept = []
    for u in range(cols):
        later = returned[u + 2 : u + 3]
        new_tables, handed = update_part(
            idx,
            came[u],
            (tables, table_moment, table_square),
            u,
            each,
            new_tables,
            kept + later,
            before,
        )
        kept = handed[: len(kept)]
        if later:
            came.append(lax.all_to_all(handed[-1], ALL, 0, 0, tiled=True))
        if counted and u == 0:
            a, b = [both_sums(x, y, 1) for x, y in zip(kept, far)]
            kept, before = [a[0], b[0]], [a[1], b[1]]
            far = [swap_peer(a[1], 2), swap_peer(b[1], 1)]
        if counted and u == 1:
            a, b = [both_sums(x, y, 0) for x, y in zip(kept, far)]
            kept, leaves = [[jnp.concatenate([x, y], axis=0)] for x, y in zip(a, b)]
            before = leaves
            far = [swap_peer(leaves[0], 4)]
        if counted and u == 2:
            state = exchange_cores(kept[0] + far[0], member)
            kept, before = [], [state[1]]
    if not counted:
        summed = lax.psum_scatter(sums[0], PEERS, scatter_dimension=0, tiled=True)
        state = exchange_cores(summed, member)
    summed = exchange_chips(state, member)
    shard_experts = (
        summed[:, :depth]
        .reshape(members, depth, mine, hidden_units)
        .swapaxes(1, 2)
        .reshape(experts, depth, hidden_units)
    )
    shard_towers, shard_gates = unpack_rows(
        jnp.sum(summed[:, depth:], axis=0),
        (tower_depth, upper_width),
        (depth, tasks * experts),
    )
    shard_towers = shard_towers.reshape(tower_depth, tasks, tower_units).swapaxes(0, 1)
    shard_gates = shard_gates.reshape(depth, tasks, experts).swapaxes(0, 1)
    same = came[1][:, each:].reshape(devices, long)
    found = []
    start = 0
    for size in cuts:
        found.append(same[:, start : start + size])
        start += size
    summed_bias = jnp.sum(found[0].reshape(2, 2, rest, halves, lots), axis=(0, 2)).reshape(
        experts, hidden_units
    )
    summed_head = jnp.sum(found[1], axis=0).reshape(head_bias.shape)
    summed_output = jnp.sum(found[2], axis=0).reshape(tower_output.shape)
    loss_sum = jnp.sum(found[3])

    return (
        *new_tables,
        *adamw(expert_weight, expert_moment, expert_square, shard_experts, dense_rate),
        *adamw(gate_weight, gate_moment, gate_square, shard_gates, dense_rate),
        *adamw(tower_weight, tower_moment, tower_square, shard_towers, dense_rate),
        *adamw(expert_bias, bias_moment, bias_square, summed_bias, dense_rate),
        *adamw(head_bias, head_moment, head_square, summed_head, dense_rate),
        *adamw(tower_output, output_moment, output_square, summed_output, dense_rate),
        loss_sum,
        weight_total,
    )


def solution(mesh):
    pieces, halves = mesh.devices.shape
    fine = Mesh(mesh.devices.reshape(2, 2, pieces // 4, halves), ALL)
    table = P(ROW, "col")
    middle = P(None, ALL, None)
    first = P(ALL)
    return jax.shard_map(
        per_device,
        mesh=fine,
        in_specs=(table,) * 3 + (middle,) * 9 + (P(),) * 9 + (first,) * 6,
        out_specs=(table,) * 3 + (middle,) * 9 + (P(),) * 11,
        check_vma=False,
    )
```

```python
import functools
import math

import jax
import jax.numpy as jnp
from jax import lax
from jax.experimental import pallas as pl
from jax.experimental.pallas import tpu as pltpu
from jax.sharding import Mesh
from jax.sharding import PartitionSpec as P

DIM = 64
STEP = 10
LANES = 128
MIB = 1024 * 1024
ROOM = 60 * MIB

beta_one = 0.9
beta_two = 0.999
epsilon = 1e-08
decay_rate = 0.01
table_rate = 0.2
dense_rate = 0.02

ROW = ("hi", "near", "rest")
PEERS = ("hi", "rest")
ALL = ("hi", "near", "rest", "col")
SCALARS = pl.BlockSpec(memory_space=pltpu.SMEM)
WHOLE = pl.BlockSpec(memory_space=pltpu.VMEM)
ANYWHERE = pl.BlockSpec(memory_space=pl.ANY)
FAR = pl.BlockSpec(memory_space=pltpu.HBM)


def adamw(weight, moment, square, gradient, rate):
    moment_next = beta_one * moment + (1.0 - beta_one) * gradient
    square_next = beta_two * square + (1.0 - beta_two) * gradient * gradient
    moment_hat = moment_next * (1.0 / (1.0 - beta_one**STEP))
    square_hat = square_next * (1.0 / (1.0 - beta_two**STEP))
    weight_next = weight - rate * (
        moment_hat / (jnp.sqrt(square_hat) + epsilon) + decay_rate * weight
    )
    return (weight_next, moment_next, square_next)


def table_adamw(weight, moment, square, gradient):
    root = math.sqrt(1.0 - beta_two**STEP)
    moment_next = beta_one * moment + (1.0 - beta_one) * gradient
    square_next = beta_two * square + (1.0 - beta_two) * (gradient * gradient)
    r = lax.rsqrt(square_next)
    below = 1.0 + (epsilon * root) * r
    near = pl.reciprocal(below, approx=True)
    near = near * (2.0 - below * near)
    ratio = (moment_next * r) * near
    weight_next = weight * (1.0 - table_rate * decay_rate) - ratio * (
        table_rate * root / (1.0 - beta_one**STEP)
    )
    return (weight_next, moment_next, square_next)


def fence(x, after):
    return pl.pallas_call(
        lambda *refs: None,
        out_shape=jax.ShapeDtypeStruct(x.shape, x.dtype),
        in_specs=[ANYWHERE] * (1 + len(after)),
        out_specs=ANYWHERE,
        input_output_aliases={0: 0},
        compiler_params=pltpu.CompilerParams(vmem_limit_bytes=MIB),
        cost_estimate=pl.CostEstimate(flops=0, bytes_accessed=0, transcendentals=0),
    )(x, *after)


def low_half():
    return lax.broadcasted_iota(jnp.int32, (1, LANES), 1) < DIM


def gather_kernel(rows, cols, devices, each, idx_ref, table_ref, out_ref, buf, sem):
    count = devices * each

    def fetch(u):
        return pltpu.make_async_copy(
            table_ref.at[:, pl.ds(u * LANES, LANES)], buf.at[u, pl.ds(0, rows)], sem.at[u]
        )

    for u in range(cols):
        fetch(u).start()
        buf[u, pl.ds(rows, 8), :] = jnp.zeros((8, LANES), jnp.float32)
    low = low_half()
    for u in range(cols):
        fetch(u).wait()

        def step(d, carry):
            base = d * each
            for k in range(each):
                first = idx_ref[2 * u * count + base + k]
                second = idx_ref[(2 * u + 1) * count + base + k]
                out_ref[d, u, pl.ds(k, 1), :] = jnp.where(
                    low, buf[u, pl.ds(first, 1), :], buf[u, pl.ds(second, 1), :]
                )
            return carry

        lax.fori_loop(0, devices, step, 0)


def gather_rows(idx, table, devices, each):
    rows, width = table.shape
    cols = width // LANES
    return pl.pallas_call(
        functools.partial(gather_kernel, rows, cols, devices, each),
        out_shape=jax.ShapeDtypeStruct((devices, cols, each, LANES), jnp.float32),
        in_specs=[SCALARS, ANYWHERE],
        out_specs=WHOLE,
        scratch_shapes=[
            pltpu.VMEM((cols, rows + 8, LANES), jnp.float32),
            pltpu.SemaphoreType.DMA((cols,)),
        ],
        compiler_params=pltpu.CompilerParams(vmem_limit_bytes=ROOM),
        cost_estimate=pl.CostEstimate(
            flops=0, bytes_accessed=2 * rows * width * 4, transcendentals=0
        ),
    )(idx, table)


def pool_kernel(pieces, halves, cols, each, place, shift_ref, peer_ref, in_ref, *refs):
    out_ref = refs[-1]
    low = low_half()
    stripe, spot = place
    for c in range(halves):
        for u in range(cols):
            shifts = [shift_ref[c * 2 * cols + 2 * u + h] for h in range(2)]
            bags = []
            for a in range(pieces // 4):
                sums = []
                for s in shifts:
                    total = None
                    for j in range(4):
                        part = in_ref[lax.rem(4 * a + j + s, pieces), c, u]
                        total = part if total is None else total + part
                    sums.append(total)
                bags.append(jnp.where(low, sums[0], sums[1]))
            at = (c * cols + u) * LANES
            block = jnp.concatenate(bags, axis=0).T
            for k in range(LANES // stripe):
                to = pl.multiple_of(spot(at // stripe + k, peer_ref[0]) * stripe, stripe)
                out_ref[pl.ds(to, stripe), :] = block[k * stripe : (k + 1) * stripe]


def pool(shifts, peer, place, arrived, before):
    pieces, halves, cols, each, _ = arrived.shape
    return pl.pallas_call(
        functools.partial(pool_kernel, pieces, halves, cols, each, place),
        out_shape=jax.ShapeDtypeStruct(
            (halves * cols * LANES, pieces // 4 * each), jnp.float32
        ),
        in_specs=[SCALARS, SCALARS, WHOLE] + [ANYWHERE] * len(before),
        out_specs=WHOLE,
        compiler_params=pltpu.CompilerParams(vmem_limit_bytes=ROOM),
    )(shifts, peer, arrived, *before)


def spread_kernel(terms, pieces, halves, cols, first, starts, each, shift_ref, *refs):
    low = low_half()
    in_refs, out_refs, rows = refs[:terms], refs[terms:-1], refs[-1]
    many = len(out_refs)
    for c in range(halves):
        for u in range(many):
            shifts = [shift_ref[c * 2 * cols + 2 * (first + u) + h] for h in range(2)]
            block = 0.0
            for ref, start in zip(in_refs, starts):
                at = start[c] + u * LANES
                block = block + ref[at : at + LANES, :]
            rows[c * many + u] = block.T
            for r in range(pieces):
                parts = []
                for s in shifts:
                    place = lax.rem(r - s + pieces, pieces) // 4
                    start = pl.multiple_of(place * each, each)
                    parts.append(rows[c * many + u, pl.ds(start, each), :])
                out_refs[u][halves * r + c] = jnp.where(low, parts[0], parts[1])


def spread(shifts, terms, starts, pieces, halves, cols, first, many):
    samples = terms[0].shape[1]
    each = samples * 4 // pieces
    return pl.pallas_call(
        functools.partial(
            spread_kernel, len(terms), pieces, halves, cols, first, starts, each
        ),
        out_shape=[
            jax.ShapeDtypeStruct((pieces * halves, each, LANES), jnp.float32)
        ]
        * many,
        in_specs=[SCALARS] + [WHOLE] * len(terms),
        out_specs=[WHOLE] * many,
        scratch_shapes=[pltpu.VMEM((halves * many, samples, LANES), jnp.float32)],
        compiler_params=pltpu.CompilerParams(vmem_limit_bytes=10 * MIB),
    )(shifts, *terms)


def update_kernel(rows, part, devices, each, block, outs, idx_ref, grad_ref, *refs):
    sources, targets = refs[:3], refs[-7 - outs : -4 - outs]
    bufs, sums, in_sem, out_sem = refs[-7:-4], refs[-4:-2], refs[-2], refs[-1]
    count = devices * each
    blocks = rows // block
    columns = pl.ds(part * LANES, LANES)

    def fetch(b, k):
        at = pl.ds(b * block, block)
        return pltpu.make_async_copy(
            sources[k].at[at, columns], bufs[k].at[at], in_sem.at[k, b]
        )

    def store(b, k):
        at = pl.ds(b * block, block)
        return pltpu.make_async_copy(
            bufs[k].at[at], targets[k].at[at, columns], out_sem.at[k, b]
        )

    for b in range(blocks):
        for k in range(3):
            fetch(b, k).start()

    def clear(i, carry):
        at = pl.ds(pl.multiple_of(i * 64, 64), 64)
        for s in sums:
            s[at, :] = jnp.full((64, LANES), jnp.inf, jnp.float32)
        return carry

    lax.fori_loop(0, rows // 64, clear, 0)
    for s in sums:
        s[pl.ds(rows, 8), :] = jnp.full((8, LANES), jnp.inf, jnp.float32)

    def step(d, carry):
        for k in range(each):
            value = grad_ref[d, pl.ds(k, 1), :]
            for q in range(2):
                row = pl.ds(idx_ref[(2 * part + q) * count + d * each + k], 1)
                old = sums[q][row, :]
                sums[q][row, :] = value + jnp.where(old < jnp.inf, old, 0.0)
        return carry

    lax.fori_loop(0, devices, step, 0)

    low = low_half()
    tile = 128
    for b in range(blocks):
        for k in range(3):
            fetch(b, k).wait()

        def renew(i, carry):
            at = pl.ds(pl.multiple_of(b * block + i * tile, tile), tile)
            total = jnp.where(low, sums[0][at, :], sums[1][at, :])
            old = [buf[at, :] for buf in bufs]
            new = table_adamw(*old, total)
            hit = total < jnp.inf
            for k in range(3):
                bufs[k][at, :] = jnp.where(hit, new[k], old[k])
            return carry

        lax.fori_loop(0, block // tile, renew, 0)
        for k in range(3):
            store(b, k).start()
    for b in range(blocks):
        for k in range(3):
            store(b, k).wait()


def update_part(idx, grads, tables, part, each, previous, through, before):
    rows, width = tables[0].shape
    devices = grads.shape[0]
    block = rows // 8
    extra = [] if previous is None else list(previous)
    place = pl.BlockSpec(memory_space=pl.ANY)
    handed = extra + list(through)
    first = 0 if extra else 3
    outs = 3 + len(through)
    done = pl.pallas_call(
        functools.partial(update_kernel, rows, part, devices, each, block, outs),
        out_shape=[jax.ShapeDtypeStruct((rows, width), jnp.float32)] * 3
        + [jax.ShapeDtypeStruct(x.shape, x.dtype) for x in through],
        in_specs=[SCALARS, WHOLE] + [place] * (3 + len(handed) + len(before)),
        out_specs=[place] * outs,
        input_output_aliases={5 + k: first + k for k in range(len(handed))},
        scratch_shapes=[pltpu.VMEM((rows, LANES), jnp.float32)] * 3
        + [pltpu.VMEM((rows + 8, LANES), jnp.float32)] * 2
        + [pltpu.SemaphoreType.DMA((3, rows // block))] * 2,
        compiler_params=pltpu.CompilerParams(vmem_limit_bytes=ROOM),
        cost_estimate=pl.CostEstimate(
            flops=30 * rows * LANES, bytes_accessed=rows * LANES * 24, transcendentals=0
        ),
    )(idx, grads, *tables, *handed, *before)
    return done[:3], list(done[3:])


GELU_SCALE = math.sqrt(2.0 / math.pi)


def gelu(a):
    return 0.5 * a * (1.0 + jnp.tanh(GELU_SCALE * (a + 0.044715 * (a * a * a))))


def gelu_slope(a):
    square = a * a
    t = jnp.tanh(GELU_SCALE * a * (1.0 + 0.044715 * square))
    return 0.5 * (1.0 + t) + (0.5 * GELU_SCALE) * a * (1.0 - t * t) * (
        1.0 + (3.0 * 0.044715) * square
    )


def split(x):
    high = x.astype(jnp.bfloat16)
    return high, (x - high.astype(jnp.float32)).astype(jnp.bfloat16)


def product(a, b, flip=False):
    dims = (((1,), (1 if flip else 0,)), ((), ()))

    def one(x, y):
        return lax.dot_general(x, y, dims, preferred_element_type=jnp.float32)

    return one(a[0], b[0]) + (one(a[0], b[1]) + one(a[1], b[0]))


TOWER_LANES = 384
GATE_LANES = 64


def pack_rows(tower, gate, width):
    def eights(x, lanes):
        x = jnp.pad(x, ((0, -x.shape[0] % 8), (0, lanes - x.shape[1])))
        return x.reshape(-1, 8, lanes).swapaxes(0, 1).reshape(8, -1)

    return padded(
        jnp.concatenate([eights(tower, TOWER_LANES), eights(gate, GATE_LANES)], axis=1), width
    )


def unpack_rows(x, tower_shape, gate_shape):
    def rows(x, shape, lanes):
        x = x.reshape(8, -1, lanes).swapaxes(0, 1).reshape(-1, lanes)
        return x[: shape[0], : shape[1]]

    cut = -(-tower_shape[0] // 8) * TOWER_LANES
    end = cut + gate_shape[0] // 8 * GATE_LANES
    return rows(x[:, :cut], tower_shape, TOWER_LANES), rows(x[:, cut:end], gate_shape, GATE_LANES)


def tower_row(order, peer_ref, number, member, tower_depth):
    rest, counted = order
    place = number ^ peer_ref[0] if counted else number
    device = ((place // rest * 2 + member // 2) * rest + place % rest) * 2 + member % 2
    row = device * tower_depth
    return pl.multiple_of(row, tower_depth) if counted else row


def split_kernel(depth, tower_depth, order, pieces, peer_ref, *refs):
    sources, far, refs = refs[:pieces], refs[pieces : pieces + 12], refs[pieces + 12 :]
    piece_refs, outs, (tower, gate, sem, out_sem) = refs[:pieces], refs[pieces:-4], refs[-4:]
    loads = [
        pltpu.make_async_copy(sources[k], piece_refs[k], sem.at[k]) for k in range(pieces)
    ]
    for load in loads:
        load.start()
    stores = [pltpu.make_async_copy(outs[k], far[k], out_sem.at[k]) for k in range(12)]

    def put(k, at, value):
        high, low = split(value)
        outs[k][at] = high
        outs[k + 1][at] = low

    block = 0
    gate_at = -(-tower_depth // 8) * TOWER_LANES
    gate[...] = jnp.zeros(gate.shape, jnp.float32)
    for load, ref in zip(loads, piece_refs):
        load.wait()
        step = min(LANES // depth, ref.shape[0])
        for b in range(0, ref.shape[0], step):
            rows = slice((block + b) * depth, (block + b + step) * depth)
            put(0, (rows, slice(None)), ref[b : b + step, :depth, :].reshape(-1, ref.shape[2]))
        for b in range(ref.shape[0]):
            number, member = (block + b) // 4, (block + b) % 4
            row = tower_row(order, peer_ref, number, member, tower_depth)
            for k in range(0, tower_depth, 8):
                high = min(8, tower_depth)
                at = k // 8 * TOWER_LANES
                tower[pl.ds(row + k, high), :] = ref[
                    b, depth : depth + high, at : at + TOWER_LANES
                ]
            for k in range(0, depth, LANES // GATE_LANES * 8):
                at = gate_at + k // 8 * GATE_LANES
                both = ref[b, depth : depth + 8, at : at + LANES]
                row = (block + b) * depth + k
                gate[row : row + 8, :GATE_LANES] = both[:, :GATE_LANES]
                if k + 8 < depth:
                    gate[row + 8 : row + 16, :GATE_LANES] = both[:, GATE_LANES:]
        block += ref.shape[0]
    for k in range(2):
        stores[k].start()
    for b in range(outs[0].shape[0] // LANES):
        rows = slice(b * LANES, (b + 1) * LANES)
        for k in range(2):
            turned = outs[k][rows, :].astype(jnp.float32).T
            outs[2 + k][:, rows] = turned.astype(jnp.bfloat16)
    width = outs[4].shape[1]
    put(4, Ellipsis, tower[:, :width])
    put(6, Ellipsis, gate[:, :GATE_LANES])
    put(8, Ellipsis, tower[...].T[:width])
    put(10, Ellipsis, gate[...].T[:GATE_LANES])
    for k in range(2, 12):
        stores[k].start()
    for store in stores:
        store.wait()


def split_weights(pieces, peer, order, depth, tower_depth, tower_width):
    lots = pieces[0].shape[2]
    devices = sum(x.shape[0] for x in pieces)
    width = devices * depth
    height = devices * tower_depth
    shapes = [(width, lots), (lots, width), (height, tower_width), (width, GATE_LANES)]
    shapes += [shapes[2][::-1], shapes[3][::-1]]
    shapes = [shape for shape in shapes for _ in range(2)]
    return pl.pallas_call(
        functools.partial(split_kernel, depth, tower_depth, order, len(pieces)),
        out_shape=[jax.ShapeDtypeStruct(shape, jnp.bfloat16) for shape in shapes],
        in_specs=[SCALARS] + [ANYWHERE] * len(pieces),
        out_specs=[FAR] * 12,
        scratch_shapes=[pltpu.VMEM(x.shape, x.dtype) for x in pieces]
        + [pltpu.VMEM(shape, jnp.bfloat16) for shape in shapes]
        + [
            pltpu.VMEM((height, TOWER_LANES), jnp.float32),
            pltpu.VMEM((width, LANES), jnp.float32),
            pltpu.SemaphoreType.DMA((len(pieces),)),
            pltpu.SemaphoreType.DMA((12,)),
        ],
        compiler_params=pltpu.CompilerParams(vmem_limit_bytes=ROOM),
    )(peer, *pieces)


def forward_kernel(dims, member_ref, *refs):
    tasks, experts, mine, hidden_units, tower_units = dims
    x_refs, weight_far, late_far = refs[:2], refs[2:4], refs[4:9]
    pre_far, upper_far, x_far, hid_far, (prob_ref, part_ref) = (
        refs[9],
        refs[10],
        refs[11:13],
        refs[13:15],
        refs[15:17],
    )
    weight, pre, upper, x, hid, late, (in_sem, out_sem, late_sem) = (
        refs[17:19],
        refs[19],
        refs[20],
        refs[21:23],
        refs[23:25],
        refs[25:30],
        refs[30:],
    )
    tower_high, tower_low, gate_high, gate_low, bias_ref = late
    lates = [pltpu.make_async_copy(late_far[k], late[k], late_sem.at[k]) for k in range(5)]
    lates[4].start()
    lots = pre.shape[0]
    tile = 256

    def load(i, k):
        at = pl.ds(i * tile, tile)
        return pltpu.make_async_copy(weight_far[k].at[at], weight[k].at[at], in_sem.at[i, k])

    for i in range(lots // tile):
        for k in range(2):
            load(i, k).start()
    for k in range(4):
        lates[k].start()
    stores = [
        pltpu.make_async_copy(a, b, out_sem.at[k])
        for k, (a, b) in enumerate(zip([*x, upper], [*x_far, upper_far]))
    ]

    def tile_stores(at):
        return [
            pltpu.make_async_copy(a.at[at], b.at[at], out_sem.at[3 + k])
            for k, (a, b) in enumerate(zip([pre, *hid], [pre_far, *hid_far]))
        ]

    for k in range(2):
        at = slice(k * LANES, (k + 1) * LANES)
        x[0][:, at], x[1][:, at] = split(x_refs[k][...])
    for k in range(2):
        stores[k].start()
    lates[4].wait()

    def rows(i, carry):
        at = pl.ds(pl.multiple_of(i * tile, tile), tile)
        for k in range(2):
            load(i, k).wait()
        value = product([w[at, :] for w in weight], [x[0][...], x[1][...]]) + bias_ref[at, :]
        pre[at, :] = value
        hid[0][at, :], hid[1][at, :] = split(gelu(value))
        for store in tile_stores(at):
            store.start()
        return carry

    lax.fori_loop(0, lots // tile, rows, 0)
    for k in range(4):
        lates[k].wait()
    logits = product([gate_high[...], gate_low[...]], [x[0][...], x[1][...]])
    total = logits.shape[1]
    logits = logits[: tasks * experts].reshape(tasks, experts, total)
    grown = jnp.exp(logits - jnp.max(logits, axis=1, keepdims=True))
    probs = grown / jnp.sum(grown, axis=1, keepdims=True)
    prob_ref[...] = probs.reshape(tasks * experts, total)
    which = lax.broadcasted_iota(jnp.int32, probs.shape, 1)
    part = jnp.zeros((tasks, tower_units, total), jnp.float32)
    for i in range(mine):
        own = jnp.sum(
            jnp.where(which == member_ref[0] * mine + i, probs, 0.0), axis=1, keepdims=True
        )
        at = slice(i * hidden_units, (i + 1) * hidden_units)
        value = product([tower_high[...], tower_low[...]], [h[at, :] for h in hid])
        upper[i] = value
        part = part + own * value.reshape(tasks, tower_units, total)
    stores[2].start()
    part = part.reshape(tasks * tower_units, total)
    part_ref[0] = part[:, :LANES]
    part_ref[1] = part[:, LANES:]
    for store in stores + tile_stores(slice(None)):
        store.wait()


def forward(dims, member, xs, weight, tower, gate, bias):
    tasks, experts, mine, hidden_units, tower_units = dims
    lots = mine * hidden_units
    width = tasks * tower_units
    total = 2 * LANES
    deep = xs[0].shape[0]
    far = [
        ((lots, total), jnp.float32),
        ((mine, width, total), jnp.float32),
        ((deep, total), jnp.bfloat16),
        ((deep, total), jnp.bfloat16),
        ((lots, total), jnp.bfloat16),
        ((lots, total), jnp.bfloat16),
    ]
    near = [((tasks * experts, total), jnp.float32), ((2, width, LANES), jnp.float32)]
    return pl.pallas_call(
        functools.partial(forward_kernel, dims),
        out_shape=[jax.ShapeDtypeStruct(*x) for x in far + near],
        in_specs=[SCALARS, WHOLE, WHOLE] + [FAR] * 7,
        out_specs=[FAR] * 6 + [WHOLE] * 2,
        scratch_shapes=[pltpu.VMEM(weight[0].shape, jnp.bfloat16)] * 2
        + [pltpu.VMEM(*x) for x in far]
        + [pltpu.VMEM(v.shape, v.dtype) for v in (*tower, *gate, bias)]
        + [
            pltpu.SemaphoreType.DMA((lots // 256, 2)),
            pltpu.SemaphoreType.DMA((6,)),
            pltpu.SemaphoreType.DMA((5,)),
        ],
        compiler_params=pltpu.CompilerParams(vmem_limit_bytes=ROOM),
        cost_estimate=pl.CostEstimate(
            flops=8 * lots * deep * total, bytes_accessed=12 * MIB, transcendentals=lots * total
        ),
    )(member, *xs, *weight, *tower, *gate, bias)


def score_kernel(
    tasks, total_ref, first_ref, second_ref, bias_ref, out_ref, last_ref, keep_ref, target_ref,
    packed_ref, grad_out_ref, grad_bias_ref, small_ref,
):
    mixed = first_ref[...] + second_ref[...]
    width, samples = mixed.shape

    def by_task(x):
        return x.reshape(tasks, width // tasks, samples)

    inner = mixed + bias_ref[...]
    upper = gelu(inner)
    keep = keep_ref[...]
    targets = target_ref[...]
    score = jnp.sum(by_task(upper * out_ref[...]), axis=1) + last_ref[...]
    faded = jnp.exp(-jnp.abs(score))
    softplus = jnp.maximum(score, 0.0) + jnp.log1p(faded)
    sigmoid = jnp.where(score >= 0.0, 1.0, faded) / (1.0 + faded)
    d_score = keep * (sigmoid - targets) / total_ref[0]
    wide = jnp.broadcast_to(d_score[:, None, :], by_task(mixed).shape).reshape(width, samples)
    d_inner = wide * out_ref[...] * gelu_slope(inner)
    packed_ref[:width, :] = d_inner
    mean = jnp.sum(by_task(d_inner * mixed), axis=1)
    packed_ref[width:, :] = jnp.concatenate(
        [mean, jnp.zeros((packed_ref.shape[0] - width - tasks, samples), jnp.float32)], axis=0
    )
    grad_out_ref[...] = jnp.sum(wide * upper, axis=1, keepdims=True)
    grad_bias_ref[...] = jnp.sum(d_inner, axis=1, keepdims=True)
    small_ref[0] = jnp.sum(d_score, axis=1, keepdims=True)
    small_ref[1] = jnp.sum(keep * (softplus - targets * score), axis=1, keepdims=True)


def score_step(tasks, weight_total, first, second, bias, out, last, keep, targets):
    width, samples = first.shape
    shapes = [(-(-(width + tasks) // 8) * 8, samples), (width, 1), (width, 1), (2, tasks, 1)]
    return pl.pallas_call(
        functools.partial(score_kernel, tasks),
        out_shape=[jax.ShapeDtypeStruct(shape, jnp.float32) for shape in shapes],
        in_specs=[SCALARS] + [WHOLE] * 7,
        out_specs=[WHOLE] * 4,
        compiler_params=pltpu.CompilerParams(vmem_limit_bytes=8 * MIB),
    )(weight_total, first, second, bias, out, last, keep, targets)


def backward_kernel(dims, place, member_ref, peer_ref, *refs):
    tasks, experts, mine, hidden_units, tower_units = dims
    stripe, spot = place
    width = tasks * tower_units
    packed_refs, prob_ref, (tower_high, tower_low, gate_high, gate_low), far_in = (
        refs[:2],
        refs[2],
        refs[3:7],
        refs[7:11],
    )
    far_out, (logit_ref, near_ref, far_ref), refs = refs[11:15], refs[15:18], refs[18:]
    pre, upper, weight, d_pre, spreads, (in_sem, out_sem) = (
        refs[0],
        refs[1],
        refs[2:4],
        refs[4:6],
        refs[6:8],
        refs[8:],
    )
    loads = [
        pltpu.make_async_copy(a, b, in_sem.at[k])
        for k, (a, b) in enumerate(zip(far_in, [upper, pre, *weight]))
    ]
    for load in loads:
        load.start()
    stores = [
        pltpu.make_async_copy(a, b, out_sem.at[k])
        for k, (a, b) in enumerate(zip([*d_pre, *spreads], far_out))
    ]
    total = 2 * LANES
    packed = jnp.concatenate([ref[...] for ref in packed_refs], axis=1)
    d_inner = packed[:width].reshape(tasks, tower_units, total)
    mean = packed[width : width + 8].reshape(1, 8, total)[0][:tasks]
    probs = prob_ref[...].reshape(tasks, experts, total)
    which = lax.broadcasted_iota(jnp.int32, probs.shape, 1)
    d_logits = jnp.zeros(probs.shape, jnp.float32)
    loads[0].wait()
    for i in range(mine):
        chosen = which == member_ref[0] * mine + i
        own = jnp.sum(jnp.where(chosen, probs, 0.0), axis=1, keepdims=True)
        d_prob = jnp.sum(d_inner * upper[i].reshape(d_inner.shape), axis=1)
        d_logit = own * (d_prob - mean)[:, None, :]
        d_logits = jnp.where(chosen, d_logit, d_logits)
        value = split((d_inner * own).reshape(width, total))
        spreads[0][i], spreads[1][i] = value
        if i == 0:
            loads[1].wait()
        at = slice(i * hidden_units, (i + 1) * hidden_units)
        d_hidden = product([tower_high[...], tower_low[...]], value)
        value = d_hidden * gelu_slope(pre[at, :])
        d_pre[0][at, :], d_pre[1][at, :] = split(value)
    for store in stores:
        store.start()
    d_logits = d_logits.reshape(tasks * experts, total)
    d_logits = jnp.concatenate(
        [d_logits, jnp.zeros((GATE_LANES - tasks * experts, total), jnp.float32)], axis=0
    )
    logit_ref[...] = d_logits
    d_logits = split(d_logits)
    for k in range(2, 4):
        loads[k].wait()
    tile = 256

    def rows(i, carry):
        at = pl.ds(pl.multiple_of(i * tile, tile), tile)
        value = product([w[at, :] for w in weight], [d_pre[0][...], d_pre[1][...]])
        value = value + product([gate_high[at, :], gate_low[at, :]], d_logits)
        for k in range(tile // stripe):
            to = pl.ds(
                pl.multiple_of(spot(i * (tile // stripe) + k, peer_ref[0]) * stripe, stripe),
                stripe,
            )
            near_ref[to, :] = value[k * stripe : (k + 1) * stripe, :LANES]
            far_ref[to, :] = value[k * stripe : (k + 1) * stripe, LANES:]
        return carry

    lax.fori_loop(0, near_ref.shape[0] // tile, rows, 0)
    for store in stores:
        store.wait()


def backward(dims, place, member, peer, packed, pre, probs, upper, weight, tower, gate):
    tasks, experts, mine, hidden_units, tower_units = dims
    lots = mine * hidden_units
    width = tasks * tower_units
    depth = weight[0].shape[0]
    total = 2 * LANES
    far = [((lots, total), jnp.bfloat16)] * 2 + [((mine, width, total), jnp.bfloat16)] * 2
    near = [
        ((GATE_LANES, total), jnp.float32),
        ((depth, LANES), jnp.float32),
        ((depth, LANES), jnp.float32),
    ]
    return pl.pallas_call(
        functools.partial(backward_kernel, dims, place),
        out_shape=[jax.ShapeDtypeStruct(*x) for x in far + near],
        in_specs=[SCALARS, SCALARS] + [WHOLE] * 7 + [FAR] * 4,
        out_specs=[FAR] * 4 + [WHOLE] * 3,
        scratch_shapes=[pltpu.VMEM(pre.shape, jnp.float32), pltpu.VMEM(upper.shape, jnp.float32)]
        + [pltpu.VMEM(weight[0].shape, jnp.bfloat16)] * 2
        + [pltpu.VMEM(*x) for x in far]
        + [pltpu.SemaphoreType.DMA((4,))] * 2,
        compiler_params=pltpu.CompilerParams(vmem_limit_bytes=ROOM),
        cost_estimate=pl.CostEstimate(
            flops=8 * lots * depth * total, bytes_accessed=12 * MIB, transcendentals=lots * total
        ),
    )(member, peer, *packed, probs, *tower, *gate, upper, pre, *weight)


def gradient_kernel(dims, depth, tower_depth, order, outs, befores, peer_ref, *refs):
    mine, hidden_units = dims
    logits, sources, refs = refs[:2], refs[2:18], refs[18 + befores :]
    weight_refs, bias_ref, refs = refs[:outs], refs[outs], refs[outs + 1 :]
    x, d_pre, hid, spreads, (tower, in_sem) = refs[:2], refs[2:4], refs[4:6], refs[6:8], refs[8:]
    half = 2 * LANES
    places = [
        pair[k].at[(Ellipsis, pl.ds(h * half, half))] if pair is not spreads else pair[k].at[h]
        for pair in (x, d_pre, hid, spreads)
        for h in range(2)
        for k in range(2)
    ]
    loads = [pltpu.make_async_copy(sources[k], places[k], in_sem.at[k]) for k in range(16)]
    for load in loads:
        load.start()
    lots = d_pre[0].shape[0]
    tile = LANES
    share = tile // depth
    tiles = x[0].shape[0] // tile
    gate_at = -(-tower_depth // 8) * TOWER_LANES
    gate_end = gate_at + depth // 8 * GATE_LANES
    for load in loads[:8]:
        load.wait()

    def parts(i):
        if outs == 1:
            return [(weight_refs[0], (), i * share, share)]
        high, middle, low = i // 4, i // 2 % 2, i % 2
        return [(weight_refs[low], (middle, high), 0, 2), (weight_refs[2 + middle], (low, high), 0, 2)]

    wide = 256

    def columns(n, carry):
        at = pl.ds(pl.multiple_of(n * wide, wide), wide)
        value = product([x[0][...], x[1][...]], [d[at, :] for d in d_pre], True)
        ones = jnp.ones((8, x[0].shape[1]), jnp.bfloat16)
        bias_ref[:, at] = sum(
            lax.dot_general(
                ones, d[at, :], (((1,), (1,)), ((), ())), preferred_element_type=jnp.float32
            )
            for d in d_pre
        )
        for i in range(tiles):
            row = i * tile
            for ref, where, first, many in parts(i):
                ref[(*where, slice(first, first + many), slice(0, depth), at)] = value[
                    row : row + many * depth
                ].reshape(many, depth, wide)
                row += many * depth
        return carry

    lax.fori_loop(0, lots // wide, columns, 0)
    d_logits = split(jnp.concatenate([ref[...] for ref in logits], axis=1))
    gates = product([x[0][...], x[1][...]], d_logits, True)
    for load in loads[8:]:
        load.wait()
    value = None
    for i in range(mine):
        for k in range(2):
            at = (slice(i * hidden_units, (i + 1) * hidden_units), slice(k * half, (k + 1) * half))
            part = product([h[at] for h in hid], [p[k, i] for p in spreads], True)
            value = part if value is None else value + part
    tower[...] = jnp.concatenate(
        [value, jnp.zeros((value.shape[0], TOWER_LANES - value.shape[1]), jnp.float32)], axis=1
    )
    full = gate_end == lots and tower_depth % 8 == 0
    for i in range(tiles):
        d = i * share
        for ref, where, first, many in parts(i):
            for k in range(first, first + many):
                if not full:
                    ref[(*where, k, slice(depth, depth + 8), slice(None))] = jnp.zeros(
                        (8, lots), jnp.float32
                    )
                row = tower_row(order, peer_ref, d // 4, d % 4, tower_depth)
                for j in range(0, tower_depth, 8):
                    high = min(8, tower_depth)
                    to = j // 8 * TOWER_LANES
                    ref[(*where, k, slice(depth, depth + high), slice(to, to + TOWER_LANES))] = (
                        tower[pl.ds(row + j, high), :]
                    )
                eights = [gates[d * depth + j : d * depth + j + 8] for j in range(0, depth, 8)]
                ref[(*where, k, slice(depth, depth + 8), slice(gate_at, gate_end))] = (
                    jnp.concatenate(eights, axis=1) if len(eights) > 1 else eights[0]
                )
                d += 1


def gradients(dims, devices, depth, tower_depth, order, peer, logits, operands, before):
    mine, hidden_units = dims
    lots = mine * hidden_units
    tall = depth + 8
    counted = order[1]
    shape = (2, 2, 2, tall, lots) if counted else (devices, tall, lots)
    outs = 4 if counted else 1
    total = 4 * LANES
    held = [(devices * depth, total), (lots, total), (lots, total), (2,) + operands[-1].shape]
    return pl.pallas_call(
        functools.partial(
            gradient_kernel, dims, depth, tower_depth, order, outs, len(before)
        ),
        out_shape=[jax.ShapeDtypeStruct(shape, jnp.float32)] * outs
        + [jax.ShapeDtypeStruct((8, lots), jnp.float32)],
        in_specs=[SCALARS, WHOLE, WHOLE] + [FAR] * 16 + [ANYWHERE] * len(before),
        out_specs=[WHOLE] * (outs + 1),
        scratch_shapes=[pltpu.VMEM(x, jnp.bfloat16) for x in held for _ in range(2)]
        + [
            pltpu.VMEM((hidden_units, TOWER_LANES), jnp.float32),
            pltpu.SemaphoreType.DMA((16,)),
        ],
        compiler_params=pltpu.CompilerParams(vmem_limit_bytes=ROOM),
        cost_estimate=pl.CostEstimate(
            flops=16 * lots * devices * depth * LANES,
            bytes_accessed=16 * MIB,
            transcendentals=0,
        ),
    )(peer, *logits, *operands, *before)


def swap_near(x):
    count = lax.axis_size("near")
    return lax.ppermute(x, "near", [(i, i ^ 1) for i in range(count)])


def swap_core(x):
    return lax.ppermute(x, "col", [(0, 1), (1, 0)])


def exchange_cores(x, member):
    blocks = [lax.dynamic_index_in_dim(x, member ^ i, 0, False) for i in range(4)]
    return blocks, swap_core(jnp.stack([blocks[1], blocks[3]]))


def exchange_chips(state, member):
    blocks, other = state
    far = swap_near(jnp.stack([blocks[2], other[1]]))
    came = jnp.stack([blocks[0], other[0], far[0], far[1]])
    return jnp.stack([lax.dynamic_index_in_dim(came, member ^ i, 0, False) for i in range(4)])


def exchange_group(x, member, after):
    blocks = [lax.dynamic_index_in_dim(x, member ^ i, 0, False) for i in range(4)]
    came = [
        blocks[0],
        swap_core(blocks[1]),
        swap_near(blocks[2]),
        lax.ppermute(blocks[3], ("near", "col"), [(i, i ^ 3) for i in range(4)]),
    ]
    came = jnp.stack(came)
    member = member + after
    return jnp.stack([lax.dynamic_index_in_dim(came, member ^ i, 0, False) for i in range(4)])


def swap_peer(x, bit):
    if bit == 4:
        return lax.ppermute(x, "hi", [(0, 1), (1, 0)])
    return lax.ppermute(x, "rest", [(i, i ^ bit) for i in range(lax.axis_size("rest"))])


def near_peers(x):
    return [swap_peer(x, bit) for bit in (1, 2, 4)]


def gather_plane(own, one, two):
    cut = own.shape[0] // 2
    return [own, one, two, swap_peer(two[:cut], 1), swap_peer(one[cut:], 2)]


def both_sums(x, far, axis):
    return [
        lax.index_in_dim(x, i, axis, False) + lax.index_in_dim(far, i, axis, False)
        for i in range(2)
    ]


def padded(x, width):
    return jnp.pad(x, [(0, 0)] * (x.ndim - 1) + [(0, width - x.shape[-1])])


def per_device(
    tables,
    table_moment,
    table_square,
    expert_weight,
    expert_moment,
    expert_square,
    gate_weight,
    gate_moment,
    gate_square,
    tower_weight,
    tower_moment,
    tower_square,
    expert_bias,
    bias_moment,
    bias_square,
    head_bias,
    head_moment,
    head_square,
    tower_output,
    output_moment,
    output_square,
    lookup_ids,
    bag_lengths,
    sample_counts,
    labels,
    label_mask,
    sample_weight,
):
    halves = lax.axis_size("col")
    rest = lax.axis_size("rest")
    pieces = 4 * rest
    devices = pieces * halves
    groups = 2 * rest
    members = devices // groups
    rows_here, width_here = tables.shape
    tabs_here = width_here // DIM
    samples, tabs, bag = lookup_ids.shape
    each = samples * bag // pieces
    classes = pieces // bag
    experts, depth, hidden_units = expert_weight.shape
    mine = experts // members
    tasks, tower_depth, tower_units = tower_weight.shape
    upper_width = tasks * tower_units
    member = lax.axis_index("near") * halves + lax.axis_index("col")
    counted = groups == 8
    peer = lax.axis_index("hi") * rest + lax.axis_index("rest") if counted else jnp.int32(0)
    peer_at = peer.astype(jnp.int32).reshape(1)
    depth = expert_weight.shape[1]

    def spot(stripe, own):
        high, near, low = stripe // (2 * rest), stripe // rest % 2, stripe % rest
        return ((high * rest + low) ^ own) * 2 + near

    def natural(stripe, own):
        number, near = (stripe // 2) ^ own, stripe % 2
        return (number // rest * 2 + near) * rest + number % rest

    place = (halves * depth, spot)
    place_back = (halves * depth, natural)

    order = (rest, counted)

    def reorder(x):
        return x.reshape((each, classes) + x.shape[1:]).swapaxes(0, 1).reshape(x.shape)

    live = (jnp.arange(samples, dtype=jnp.int32) < sample_counts[0]).astype(jnp.float32)
    keep = reorder(sample_weight[:, None] * label_mask.astype(jnp.float32) * live[:, None])
    targets = reorder(labels.astype(jnp.float32))

    ids = lookup_ids.transpose(0, 2, 1).reshape(each, pieces, tabs)
    use = jnp.arange(bag, dtype=jnp.int32)[None, :, None] < bag_lengths[:, None, :]
    owner = ids // rows_here
    local = jnp.where(use.reshape(each, pieces, tabs), ids - owner * rows_here, rows_here)
    here = owner[None] == jnp.arange(pieces, dtype=jnp.int32)[:, None, None, None]
    wanted = jnp.sum(jnp.where(here, local[None], 0), axis=2)
    wanted = wanted.transpose(0, 2, 1).reshape(devices, tabs_here * each).astype(jnp.float32)
    message = jnp.concatenate(
        [wanted, jnp.broadcast_to(jnp.sum(keep), (devices, 1))], axis=1
    )
    wide = -(-message.shape[1] // 1024) * 1024
    message = padded(message, wide).reshape(devices, wide // LANES, LANES)
    shifts = lookup_ids[0, :, 0] // rows_here

    lots = mine * hidden_units
    send = expert_weight.reshape(members, mine, depth, hidden_units).swapaxes(1, 2)
    send = send.reshape(members, depth, lots)
    small = pack_rows(
        tower_weight.swapaxes(0, 1).reshape(tower_depth, upper_width),
        gate_weight.swapaxes(0, 1).reshape(depth, tasks * experts),
        lots,
    )
    send = jnp.concatenate(
        [send, jnp.broadcast_to(small[None], (members,) + small.shape)], axis=1
    )
    asked = lax.all_to_all(message, ALL, 0, 0, tiled=True).reshape(devices, wide)
    idx = asked[:, : tabs_here * each].reshape(devices, tabs_here, each)
    idx = idx.swapaxes(0, 1).reshape(-1).astype(jnp.int32)
    weight_total = jnp.sum(asked[:, tabs_here * each])

    shared = exchange_group(send, member, jnp.minimum(idx[0], 0))
    if counted:
        one, two, top = near_peers(shared)
        parts = gather_plane(shared, one, two)
        early = [one, two, top]
        parts += gather_plane(top, swap_peer(top, 1), swap_peer(top, 2))
    else:
        early = [shared]
        parts = [lax.all_gather(shared, PEERS, axis=0, tiled=True)]
    bias_mine = lax.dynamic_slice_in_dim(expert_bias, member * mine, mine, 0).reshape(lots, 1)

    picked = fence(gather_rows(idx, tables, devices, each), early)
    cols = width_here // LANES
    arrived = lax.all_to_all(
        picked.reshape(devices, cols * each, LANES), ALL, 0, 0, tiled=True
    ).reshape(pieces, halves, cols, each, LANES)
    split_parts = split_weights(
        parts, peer_at, order, depth, tower_depth, upper_width
    )
    weight_pair, weight_turned, tower_pair, gate_pair, tower_turned, gate_turned = [
        split_parts[2 * k : 2 * k + 2] for k in range(6)
    ]
    mine_x = pool(shifts, peer_at, place, arrived, parts)
    near_x = swap_near(mine_x)
    halves_x = [(mine_x, swap_core(mine_x))]

    dims = (tasks, experts, mine, hidden_units, tower_units)
    member_at = member.astype(jnp.int32).reshape(1)
    def half_forward(x):
        return forward(
            dims, member_at, x, weight_turned, tower_turned, gate_turned, bias_mine
        )

    runs = [half_forward(halves_x[0])]
    near_x = fence(near_x, [runs[0][7]])
    halves_x.append((near_x, swap_core(near_x)))
    runs.append(half_forward(halves_x[1]))
    part_own, part_near = runs[0][7], runs[1][7]
    first = part_own[0] + swap_core(part_own[1])
    second = swap_near(part_near[0] + swap_core(part_near[1]))
    packed, grad_output, grad_head, few = score_step(
        tasks,
        weight_total.reshape(1),
        first,
        second,
        head_bias[:, :-1].reshape(upper_width, 1),
        tower_output.reshape(upper_width, 1),
        head_bias[:, -1:],
        keep.T,
        targets.T,
    )

    core_packed = swap_core(packed)
    halves_packed = [(packed, core_packed), (swap_near(packed), swap_near(core_packed))]

    def half_back(k, packed):
        run = runs[k]
        return backward(
            dims,
            place_back,
            member_at,
            peer_at,
            packed,
            run[0],
            run[6],
            run[1],
            weight_pair,
            tower_pair,
            gate_pair,
        )

    back = [half_back(0, halves_packed[0])]
    near_first, near_second = halves_packed[1]
    back.append(half_back(1, (fence(near_first, [back[0][4]]), near_second)))
    near_in, far_in = back[1][5:]
    leaving = near_in + swap_core(far_in)

    half_width = width_here
    ahead = jnp.concatenate(
        [leaving[c * half_width : c * half_width + LANES] for c in range(halves)], axis=0
    )
    others = jnp.concatenate(
        [leaving[c * half_width + LANES : (c + 1) * half_width] for c in range(halves)], axis=0
    )
    ahead = swap_near(ahead)
    others = swap_near(others)
    terms = [back[0][5], swap_core(back[0][6])]

    def starts(first, stride):
        whole = tuple(c * half_width + first for c in range(halves))
        return (whole, whole, tuple(c * stride for c in range(halves)))

    returned = list(
        spread(shifts, terms + [ahead], starts(0, LANES), pieces, halves, cols, 0, 1)
    )
    returned += list(
        spread(
            shifts,
            terms + [fence(others, returned)],
            starts(LANES, half_width - LANES),
            pieces,
            halves,
            cols,
            1,
            cols - 1,
        )
    )

    *sums, grad_bias = gradients(
        (mine, hidden_units),
        devices,
        depth,
        tower_depth,
        order,
        peer_at,
        [x[4] for x in back],
        [x[k] for x in runs for k in (2, 3)]
        + [x[k] for x in back for k in (0, 1)]
        + [x[k] for x in runs for k in (4, 5)]
        + [x[k] for x in back for k in (2, 3)],
        [returned[0], others],
    )

    grad_head = jnp.concatenate([grad_head.reshape(tasks, tower_units), few[0]], axis=1)
    same = jnp.concatenate(
        [
            grad_bias[0],
            grad_head.reshape(-1),
            grad_output.reshape(-1),
            jnp.sum(few[1]).reshape(1),
        ]
    )
    cuts = [lots, grad_head.size, grad_output.size, 1]
    long = -(-same.shape[0] // 1024) * 1024
    same = jnp.broadcast_to(
        padded(same, long).reshape(1, long // LANES, LANES), (devices, long // LANES, LANES)
    )
    returned[1] = jnp.concatenate([returned[1], same], axis=1)
    came = [lax.all_to_all(x, ALL, 0, 0, tiled=True) for x in returned[:2]]
    new_tables = None
    before = []
    if counted:
        kept = [sums[0], sums[2]]
        far = [swap_peer(sums[1], 1), swap_peer(sums[3], 2)]
    else:
        kept = []
    for u in range(cols):
        later = returned[2:] if u == 0 else []
        new_tables, handed = update_part(
            idx,
            came[u],
            (tables, table_moment, table_square),
            u,
            each,
            new_tables,
            kept + later,
            before,
        )
        kept = handed[: len(kept)]
        if later:
            came += [
                lax.all_to_all(x, ALL, 0, 0, tiled=True) for x in handed[len(handed) - len(later) :]
            ]
        if counted and u == 0:
            a, b = [both_sums(x, y, 0) for x, y in zip(kept, far)]
            kept, before = [a[0], b[0]], [a[1], b[1]]
            far = [swap_peer(a[1], 2), swap_peer(b[1], 1)]
        if counted and u == 1:
            a, b = [both_sums(x, y, 0) for x, y in zip(kept, far)]
            kept, leaves = [[jnp.concatenate([x, y], axis=0)] for x, y in zip(a, b)]
            before = leaves
            far = [swap_peer(leaves[0], 4)]
        if counted and u == 2:
            state = exchange_cores(kept[0] + far[0], member)
            kept, before = [], [state[1]]
    if not counted:
        summed = lax.psum_scatter(sums[0], PEERS, scatter_dimension=0, tiled=True)
        state = exchange_cores(summed, member)
    summed = exchange_chips(state, member)
    shard_experts = (
        summed[:, :depth]
        .reshape(members, depth, mine, hidden_units)
        .swapaxes(1, 2)
        .reshape(experts, depth, hidden_units)
    )
    shard_towers, shard_gates = unpack_rows(
        jnp.sum(summed[:, depth:], axis=0),
        (tower_depth, upper_width),
        (depth, tasks * experts),
    )
    shard_towers = shard_towers.reshape(tower_depth, tasks, tower_units).swapaxes(0, 1)
    shard_gates = shard_gates.reshape(depth, tasks, experts).swapaxes(0, 1)
    same = came[1][:, each:].reshape(devices, long)
    found = []
    start = 0
    for size in cuts:
        found.append(same[:, start : start + size])
        start += size
    summed_bias = jnp.sum(found[0].reshape(2, 2, rest, halves, lots), axis=(0, 2)).reshape(
        experts, hidden_units
    )
    summed_head = jnp.sum(found[1], axis=0).reshape(head_bias.shape)
    summed_output = jnp.sum(found[2], axis=0).reshape(tower_output.shape)
    loss_sum = jnp.sum(found[3])

    return (
        *new_tables,
        *adamw(expert_weight, expert_moment, expert_square, shard_experts, dense_rate),
        *adamw(gate_weight, gate_moment, gate_square, shard_gates, dense_rate),
        *adamw(tower_weight, tower_moment, tower_square, shard_towers, dense_rate),
        *adamw(expert_bias, bias_moment, bias_square, summed_bias, dense_rate),
        *adamw(head_bias, head_moment, head_square, summed_head, dense_rate),
        *adamw(tower_output, output_moment, output_square, summed_output, dense_rate),
        loss_sum,
        weight_total,
    )


def solution(mesh):
    pieces, halves = mesh.devices.shape
    fine = Mesh(mesh.devices.reshape(2, 2, pieces // 4, halves), ALL)
    table = P(ROW, "col")
    middle = P(None, ALL, None)
    first = P(ALL)
    return jax.shard_map(
        per_device,
        mesh=fine,
        in_specs=(table,) * 3 + (middle,) * 9 + (P(),) * 9 + (first,) * 6,
        out_specs=(table,) * 3 + (middle,) * 9 + (P(),) * 11,
        check_vma=False,
    )
```

```python
import functools
import math

import jax
import jax.numpy as jnp
from jax import lax
from jax.experimental import pallas as pl
from jax.experimental.pallas import tpu as pltpu
from jax.sharding import Mesh
from jax.sharding import PartitionSpec as P

DIM = 64
STEP = 10
LANES = 128
MIB = 1024 * 1024
ROOM = 60 * MIB

beta_one = 0.9
beta_two = 0.999
epsilon = 1e-08
decay_rate = 0.01
table_rate = 0.2
dense_rate = 0.02

ROW = ("hi", "near", "rest")
PEERS = ("hi", "rest")
ALL = ("hi", "near", "rest", "col")
SCALARS = pl.BlockSpec(memory_space=pltpu.SMEM)
WHOLE = pl.BlockSpec(memory_space=pltpu.VMEM)
ANYWHERE = pl.BlockSpec(memory_space=pl.ANY)
FAR = pl.BlockSpec(memory_space=pltpu.HBM)


def adamw(weight, moment, square, gradient, rate):
    moment_next = beta_one * moment + (1.0 - beta_one) * gradient
    square_next = beta_two * square + (1.0 - beta_two) * gradient * gradient
    moment_hat = moment_next * (1.0 / (1.0 - beta_one**STEP))
    square_hat = square_next * (1.0 / (1.0 - beta_two**STEP))
    weight_next = weight - rate * (
        moment_hat / (jnp.sqrt(square_hat) + epsilon) + decay_rate * weight
    )
    return (weight_next, moment_next, square_next)


def table_adamw(weight, moment, square, gradient):
    root = math.sqrt(1.0 - beta_two**STEP)
    moment_next = beta_one * moment + (1.0 - beta_one) * gradient
    square_next = beta_two * square + (1.0 - beta_two) * (gradient * gradient)
    r = lax.rsqrt(square_next)
    below = 1.0 + (epsilon * root) * r
    near = pl.reciprocal(below, approx=True)
    near = near * (2.0 - below * near)
    ratio = (moment_next * r) * near
    weight_next = weight * (1.0 - table_rate * decay_rate) - ratio * (
        table_rate * root / (1.0 - beta_one**STEP)
    )
    return (weight_next, moment_next, square_next)


def fence(x, after, room=MIB):
    return pl.pallas_call(
        lambda *refs: None,
        out_shape=jax.ShapeDtypeStruct(x.shape, x.dtype),
        in_specs=[ANYWHERE] * (1 + len(after)),
        out_specs=ANYWHERE,
        input_output_aliases={0: 0},
        compiler_params=pltpu.CompilerParams(vmem_limit_bytes=room),
        cost_estimate=pl.CostEstimate(flops=0, bytes_accessed=0, transcendentals=0),
    )(x, *after)


def low_half():
    return lax.broadcasted_iota(jnp.int32, (1, LANES), 1) < DIM


def gather_kernel(rows, cols, devices, each, idx_ref, table_ref, far_ref, buf, out_ref, sem, out_sem):
    count = devices * each

    def fetch(u):
        return pltpu.make_async_copy(
            table_ref.at[:, pl.ds(u * LANES, LANES)], buf.at[u, pl.ds(0, rows)], sem.at[u]
        )

    for u in range(cols):
        fetch(u).start()
        buf[u, pl.ds(rows, 8), :] = jnp.zeros((8, LANES), jnp.float32)
    low = low_half()
    for u in range(cols):
        fetch(u).wait()

        def step(d, carry):
            base = d * each
            for k in range(each):
                first = idx_ref[2 * u * count + base + k]
                second = idx_ref[(2 * u + 1) * count + base + k]
                out_ref[d, u, pl.ds(k, 1), :] = jnp.where(
                    low, buf[u, pl.ds(first, 1), :], buf[u, pl.ds(second, 1), :]
                )
            return carry

        lax.fori_loop(0, devices, step, 0)
        pltpu.make_async_copy(out_ref.at[:, u], far_ref.at[:, u], out_sem.at[u]).start()
    for u in range(cols):
        pltpu.make_async_copy(out_ref.at[:, u], far_ref.at[:, u], out_sem.at[u]).wait()


def gather_rows(idx, table, devices, each):
    rows, width = table.shape
    cols = width // LANES
    return pl.pallas_call(
        functools.partial(gather_kernel, rows, cols, devices, each),
        out_shape=jax.ShapeDtypeStruct((devices, cols, each, LANES), jnp.float32),
        in_specs=[SCALARS, ANYWHERE],
        out_specs=FAR,
        scratch_shapes=[
            pltpu.VMEM((cols, rows + 8, LANES), jnp.float32),
            pltpu.VMEM((devices, cols, each, LANES), jnp.float32),
            pltpu.SemaphoreType.DMA((cols,)),
            pltpu.SemaphoreType.DMA((cols,)),
        ],
        compiler_params=pltpu.CompilerParams(vmem_limit_bytes=ROOM),
        cost_estimate=pl.CostEstimate(
            flops=0, bytes_accessed=2 * rows * width * 4, transcendentals=0
        ),
    )(idx, table)


def pool_kernel(pieces, halves, cols, each, place, shift_ref, peer_ref, in_ref, *refs):
    out_ref = refs[-1]
    low = low_half()
    stripe, spot = place
    for c in range(halves):
        for u in range(cols):
            shifts = [shift_ref[c * 2 * cols + 2 * u + h] for h in range(2)]
            bags = []
            for a in range(pieces // 4):
                sums = []
                for s in shifts:
                    total = None
                    for j in range(4):
                        part = in_ref[lax.rem(4 * a + j + s, pieces), c, u]
                        total = part if total is None else total + part
                    sums.append(total)
                bags.append(jnp.where(low, sums[0], sums[1]))
            at = (c * cols + u) * LANES
            block = jnp.concatenate(bags, axis=0).T
            for k in range(LANES // stripe):
                to = pl.multiple_of(spot(at // stripe + k, peer_ref[0]) * stripe, stripe)
                out_ref[pl.ds(to, stripe), :] = block[k * stripe : (k + 1) * stripe]


def pool(shifts, peer, place, arrived, before):
    pieces, halves, cols, each, _ = arrived.shape
    return pl.pallas_call(
        functools.partial(pool_kernel, pieces, halves, cols, each, place),
        out_shape=jax.ShapeDtypeStruct(
            (halves * cols * LANES, pieces // 4 * each), jnp.float32
        ),
        in_specs=[SCALARS, SCALARS, WHOLE] + [ANYWHERE] * len(before),
        out_specs=WHOLE,
        compiler_params=pltpu.CompilerParams(vmem_limit_bytes=ROOM),
    )(shifts, peer, arrived, *before)


def spread_kernel(terms, pieces, halves, cols, first, starts, each, shift_ref, *refs):
    low = low_half()
    in_refs, out_refs, rows = refs[:terms], refs[terms:-1], refs[-1]
    many = len(out_refs)
    for c in range(halves):
        for u in range(many):
            shifts = [shift_ref[c * 2 * cols + 2 * (first + u) + h] for h in range(2)]
            block = 0.0
            for ref, start in zip(in_refs, starts):
                at = start[c] + u * LANES
                block = block + ref[at : at + LANES, :]
            rows[c * many + u] = block.T
            for r in range(pieces):
                parts = []
                for s in shifts:
                    place = lax.rem(r - s + pieces, pieces) // 4
                    start = pl.multiple_of(place * each, each)
                    parts.append(rows[c * many + u, pl.ds(start, each), :])
                out_refs[u][halves * r + c] = jnp.where(low, parts[0], parts[1])


def spread(shifts, terms, starts, pieces, halves, cols, first, many):
    samples = terms[0].shape[1]
    each = samples * 4 // pieces
    return pl.pallas_call(
        functools.partial(
            spread_kernel, len(terms), pieces, halves, cols, first, starts, each
        ),
        out_shape=[
            jax.ShapeDtypeStruct((pieces * halves, each, LANES), jnp.float32)
        ]
        * many,
        in_specs=[SCALARS] + [WHOLE] * len(terms),
        out_specs=[WHOLE] * many,
        scratch_shapes=[pltpu.VMEM((halves * many, samples, LANES), jnp.float32)],
        compiler_params=pltpu.CompilerParams(vmem_limit_bytes=10 * MIB),
    )(shifts, *terms)


def update_kernel(rows, part, devices, each, block, outs, idx_ref, grad_ref, *refs):
    sources, targets = refs[:3], refs[-7 - outs : -4 - outs]
    bufs, sums, in_sem, out_sem = refs[-7:-4], refs[-4:-2], refs[-2], refs[-1]
    count = devices * each
    blocks = rows // block
    columns = pl.ds(part * LANES, LANES)

    def fetch(b, k):
        at = pl.ds(b * block, block)
        return pltpu.make_async_copy(
            sources[k].at[at, columns], bufs[k].at[at], in_sem.at[k, b]
        )

    def store(b, k):
        at = pl.ds(b * block, block)
        return pltpu.make_async_copy(
            bufs[k].at[at], targets[k].at[at, columns], out_sem.at[k, b]
        )

    for b in range(blocks):
        for k in range(3):
            fetch(b, k).start()

    def clear(i, carry):
        at = pl.ds(pl.multiple_of(i * 64, 64), 64)
        for s in sums:
            s[at, :] = jnp.full((64, LANES), jnp.inf, jnp.float32)
        return carry

    lax.fori_loop(0, rows // 64, clear, 0)
    for s in sums:
        s[pl.ds(rows, 8), :] = jnp.full((8, LANES), jnp.inf, jnp.float32)

    def step(d, carry):
        for k in range(each):
            value = grad_ref[d, pl.ds(k, 1), :]
            for q in range(2):
                row = pl.ds(idx_ref[(2 * part + q) * count + d * each + k], 1)
                old = sums[q][row, :]
                sums[q][row, :] = value + jnp.where(old < jnp.inf, old, 0.0)
        return carry

    lax.fori_loop(0, devices, step, 0)

    low = low_half()
    tile = 128
    for b in range(blocks):
        for k in range(3):
            fetch(b, k).wait()

        def renew(i, carry):
            at = pl.ds(pl.multiple_of(b * block + i * tile, tile), tile)
            total = jnp.where(low, sums[0][at, :], sums[1][at, :])
            old = [buf[at, :] for buf in bufs]
            new = table_adamw(*old, total)
            hit = total < jnp.inf
            for k in range(3):
                bufs[k][at, :] = jnp.where(hit, new[k], old[k])
            return carry

        lax.fori_loop(0, block // tile, renew, 0)
        for k in range(3):
            store(b, k).start()
    for b in range(blocks):
        for k in range(3):
            store(b, k).wait()


def update_part(idx, grads, tables, part, each, previous, through, before):
    rows, width = tables[0].shape
    devices = grads.shape[0]
    block = rows // 8
    extra = [] if previous is None else list(previous)
    place = pl.BlockSpec(memory_space=pl.ANY)
    handed = extra + list(through)
    first = 0 if extra else 3
    outs = 3 + len(through)
    done = pl.pallas_call(
        functools.partial(update_kernel, rows, part, devices, each, block, outs),
        out_shape=[jax.ShapeDtypeStruct((rows, width), jnp.float32)] * 3
        + [jax.ShapeDtypeStruct(x.shape, x.dtype) for x in through],
        in_specs=[SCALARS, WHOLE] + [place] * (3 + len(handed) + len(before)),
        out_specs=[place] * outs,
        input_output_aliases={5 + k: first + k for k in range(len(handed))},
        scratch_shapes=[pltpu.VMEM((rows, LANES), jnp.float32)] * 3
        + [pltpu.VMEM((rows + 8, LANES), jnp.float32)] * 2
        + [pltpu.SemaphoreType.DMA((3, rows // block))] * 2,
        compiler_params=pltpu.CompilerParams(vmem_limit_bytes=ROOM),
        cost_estimate=pl.CostEstimate(
            flops=30 * rows * LANES, bytes_accessed=rows * LANES * 24, transcendentals=0
        ),
    )(idx, grads, *tables, *handed, *before)
    return done[:3], list(done[3:])


GELU_SCALE = math.sqrt(2.0 / math.pi)


def gelu(a):
    return 0.5 * a * (1.0 + jnp.tanh(GELU_SCALE * (a + 0.044715 * (a * a * a))))


def gelu_slope(a):
    square = a * a
    t = jnp.tanh(GELU_SCALE * a * (1.0 + 0.044715 * square))
    return 0.5 * (1.0 + t) + (0.5 * GELU_SCALE) * a * (1.0 - t * t) * (
        1.0 + (3.0 * 0.044715) * square
    )


def split(x):
    high = x.astype(jnp.bfloat16)
    return high, (x - high.astype(jnp.float32)).astype(jnp.bfloat16)


def product(a, b, flip=False):
    dims = (((1,), (1 if flip else 0,)), ((), ()))

    def one(x, y):
        return lax.dot_general(x, y, dims, preferred_element_type=jnp.float32)

    return one(a[0], b[0]) + (one(a[0], b[1]) + one(a[1], b[0]))


TOWER_LANES = 384
GATE_LANES = 64


def pack_rows(tower, gate, width):
    def eights(x, lanes):
        x = jnp.pad(x, ((0, -x.shape[0] % 8), (0, lanes - x.shape[1])))
        return x.reshape(-1, 8, lanes).swapaxes(0, 1).reshape(8, -1)

    return padded(
        jnp.concatenate([eights(tower, TOWER_LANES), eights(gate, GATE_LANES)], axis=1), width
    )


def unpack_rows(x, tower_shape, gate_shape):
    def rows(x, shape, lanes):
        x = x.reshape(8, -1, lanes).swapaxes(0, 1).reshape(-1, lanes)
        return x[: shape[0], : shape[1]]

    cut = -(-tower_shape[0] // 8) * TOWER_LANES
    end = cut + gate_shape[0] // 8 * GATE_LANES
    return rows(x[:, :cut], tower_shape, TOWER_LANES), rows(x[:, cut:end], gate_shape, GATE_LANES)


def tower_row(order, peer_ref, number, member, tower_depth):
    rest, counted = order
    place = number ^ peer_ref[0] if counted else number
    device = ((place // rest * 2 + member // 2) * rest + place % rest) * 2 + member % 2
    row = device * tower_depth
    return pl.multiple_of(row, tower_depth) if counted else row


def split_kernel(depth, tower_depth, order, sizes, befores, turn, peer_ref, *refs):
    pieces = len(sizes)
    sources, refs = refs[:pieces], refs[pieces + befores :]
    far, (whole, *outs), (tower, gate, sem, out_sem) = refs[:6], refs[6:13], refs[13:]
    loads = []
    ends = []
    for k in range(pieces):
        start = sum(sizes[:k])
        loads.append(
            pltpu.make_async_copy(sources[k], whole.at[pl.ds(start, sizes[k])], sem.at[k])
        )
        ends.append(start + sizes[k])
    for load in loads:
        load.start()
    gate_at = -(-tower_depth // 8) * TOWER_LANES
    gate[...] = jnp.zeros(gate.shape, jnp.float32)
    devices, _, lots = whole.shape
    share = LANES // depth
    waited = 0
    stores = []

    def store(k, at, n):
        copy = pltpu.make_async_copy(outs[k].at[at], far[k].at[at], out_sem.at[k, n])
        copy.start()
        stores.append(copy)

    for n in range(devices // share):
        while waited < pieces and (waited == 0 or ends[waited - 1] < (n + 1) * share):
            loads[waited].wait()
            waited += 1
        rows = slice(n * LANES, (n + 1) * LANES)
        block = whole[n * share : (n + 1) * share, :depth, :].reshape(LANES, lots)
        at = (slice(None), rows) if turn else (rows, slice(None))
        outs[0][at], outs[1][at] = split(block.T if turn else block)
        for k in range(2):
            store(k, at, n)
        for d in range(n * share, (n + 1) * share):
            row = tower_row(order, peer_ref, d // 4, d % 4, tower_depth)
            for k in range(0, tower_depth, 8):
                high = min(8, tower_depth)
                at = k // 8 * TOWER_LANES
                tower[pl.ds(row + k, high), :] = whole[
                    d, depth : depth + high, at : at + TOWER_LANES
                ]
            for k in range(0, depth, LANES // GATE_LANES * 8):
                at = gate_at + k // 8 * GATE_LANES
                both = whole[d, depth : depth + 8, at : at + LANES]
                row = d * depth + k
                gate[row : row + 8, :GATE_LANES] = both[:, :GATE_LANES]
                if k + 8 < depth:
                    gate[row + 8 : row + 16, :GATE_LANES] = both[:, GATE_LANES:]
    if turn:
        width = outs[2].shape[0]
        outs[2][...], outs[3][...] = split(tower[...].T[:width])
        outs[4][...], outs[5][...] = split(gate[...].T[:GATE_LANES])
    else:
        width = outs[2].shape[1]
        outs[2][...], outs[3][...] = split(tower[:, :width])
        outs[4][...], outs[5][...] = split(gate[:, :GATE_LANES])
    for k in range(2, 6):
        store(k, Ellipsis, 0)
    for copy in stores:
        copy.wait()


def split_weights(pieces, peer, order, depth, tower_depth, tower_width, turn, before):
    lots = pieces[0].shape[2]
    sizes = tuple(x.shape[0] for x in pieces)
    devices = sum(sizes)
    width = devices * depth
    height = devices * tower_depth
    shapes = [(width, lots), (height, tower_width), (width, GATE_LANES)]
    shapes = [shape[::-1] if turn else shape for shape in shapes for _ in range(2)]
    done = pl.pallas_call(
        functools.partial(
            split_kernel, depth, tower_depth, order, sizes, len(before), turn
        ),
        out_shape=[jax.ShapeDtypeStruct(shape, jnp.bfloat16) for shape in shapes],
        in_specs=[SCALARS] + [ANYWHERE] * (len(pieces) + len(before)),
        out_specs=[FAR] * 6,
        scratch_shapes=[pltpu.VMEM((devices,) + pieces[0].shape[1:], jnp.float32)]
        + [pltpu.VMEM(shape, jnp.bfloat16) for shape in shapes]
        + [
            pltpu.VMEM((height, TOWER_LANES), jnp.float32),
            pltpu.VMEM((width, LANES), jnp.float32),
            pltpu.SemaphoreType.DMA((len(pieces),)),
            pltpu.SemaphoreType.DMA((6, width // LANES)),
        ],
        compiler_params=pltpu.CompilerParams(vmem_limit_bytes=ROOM),
    )(peer, *pieces, *before)
    return [done[2 * k : 2 * k + 2] for k in range(3)]


def forward_kernel(dims, member_ref, *refs):
    tasks, experts, mine, hidden_units, tower_units = dims
    x_refs, weight_far, late_far = refs[:2], refs[2:4], refs[4:9]
    pre_far, upper_far, x_far, hid_far, (prob_ref, part_ref) = (
        refs[9],
        refs[10],
        refs[11:13],
        refs[13:15],
        refs[15:17],
    )
    weight, pre, upper, x, hid, late, (in_sem, out_sem, late_sem) = (
        refs[17:19],
        refs[19],
        refs[20],
        refs[21:23],
        refs[23:25],
        refs[25:30],
        refs[30:],
    )
    tower_high, tower_low, gate_high, gate_low, bias_ref = late
    lates = [pltpu.make_async_copy(late_far[k], late[k], late_sem.at[k]) for k in range(5)]
    lates[4].start()
    lots = pre.shape[0]
    tile = 256

    def load(i, k):
        at = pl.ds(i * tile, tile)
        return pltpu.make_async_copy(weight_far[k].at[at], weight[k].at[at], in_sem.at[i, k])

    for i in range(lots // tile):
        for k in range(2):
            load(i, k).start()
    for k in range(4):
        lates[k].start()
    stores = [
        pltpu.make_async_copy(a, b, out_sem.at[k])
        for k, (a, b) in enumerate(zip([*x, upper], [*x_far, upper_far]))
    ]

    def tile_stores(at):
        return [
            pltpu.make_async_copy(a.at[at], b.at[at], out_sem.at[3 + k])
            for k, (a, b) in enumerate(zip([pre, *hid], [pre_far, *hid_far]))
        ]

    for k in range(2):
        at = slice(k * LANES, (k + 1) * LANES)
        x[0][:, at], x[1][:, at] = split(x_refs[k][...])
    for k in range(2):
        stores[k].start()
    lates[4].wait()

    def rows(i, carry):
        at = pl.ds(pl.multiple_of(i * tile, tile), tile)
        for k in range(2):
            load(i, k).wait()
        value = product([w[at, :] for w in weight], [x[0][...], x[1][...]]) + bias_ref[at, :]
        pre[at, :] = value
        hid[0][at, :], hid[1][at, :] = split(gelu(value))
        for store in tile_stores(at):
            store.start()
        return carry

    lax.fori_loop(0, lots // tile, rows, 0)
    for k in range(4):
        lates[k].wait()
    logits = product([gate_high[...], gate_low[...]], [x[0][...], x[1][...]])
    total = logits.shape[1]
    logits = logits[: tasks * experts].reshape(tasks, experts, total)
    grown = jnp.exp(logits - jnp.max(logits, axis=1, keepdims=True))
    probs = grown / jnp.sum(grown, axis=1, keepdims=True)
    prob_ref[...] = probs.reshape(tasks * experts, total)
    which = lax.broadcasted_iota(jnp.int32, probs.shape, 1)
    part = jnp.zeros((tasks, tower_units, total), jnp.float32)
    for i in range(mine):
        own = jnp.sum(
            jnp.where(which == member_ref[0] * mine + i, probs, 0.0), axis=1, keepdims=True
        )
        at = slice(i * hidden_units, (i + 1) * hidden_units)
        value = product([tower_high[...], tower_low[...]], [h[at, :] for h in hid])
        upper[i] = value
        part = part + own * value.reshape(tasks, tower_units, total)
    stores[2].start()
    part = part.reshape(tasks * tower_units, total)
    part_ref[0] = part[:, :LANES]
    part_ref[1] = part[:, LANES:]
    for store in stores + tile_stores(slice(None)):
        store.wait()


def forward(dims, member, xs, weight, tower, gate, bias):
    tasks, experts, mine, hidden_units, tower_units = dims
    lots = mine * hidden_units
    width = tasks * tower_units
    total = 2 * LANES
    deep = xs[0].shape[0]
    far = [
        ((lots, total), jnp.float32),
        ((mine, width, total), jnp.float32),
        ((deep, total), jnp.bfloat16),
        ((deep, total), jnp.bfloat16),
        ((lots, total), jnp.bfloat16),
        ((lots, total), jnp.bfloat16),
    ]
    near = [((tasks * experts, total), jnp.float32), ((2, width, LANES), jnp.float32)]
    return pl.pallas_call(
        functools.partial(forward_kernel, dims),
        out_shape=[jax.ShapeDtypeStruct(*x) for x in far + near],
        in_specs=[SCALARS, WHOLE, WHOLE] + [FAR] * 7,
        out_specs=[FAR] * 6 + [WHOLE] * 2,
        scratch_shapes=[pltpu.VMEM(weight[0].shape, jnp.bfloat16)] * 2
        + [pltpu.VMEM(*x) for x in far]
        + [pltpu.VMEM(v.shape, v.dtype) for v in (*tower, *gate, bias)]
        + [
            pltpu.SemaphoreType.DMA((lots // 256, 2)),
            pltpu.SemaphoreType.DMA((6,)),
            pltpu.SemaphoreType.DMA((5,)),
        ],
        compiler_params=pltpu.CompilerParams(vmem_limit_bytes=ROOM),
        cost_estimate=pl.CostEstimate(
            flops=8 * lots * deep * total, bytes_accessed=12 * MIB, transcendentals=lots * total
        ),
    )(member, *xs, *weight, *tower, *gate, bias)


def score_kernel(
    tasks, total_ref, first_ref, second_ref, bias_ref, out_ref, last_ref, keep_ref, target_ref,
    before, packed_ref, grad_out_ref, grad_bias_ref, small_ref,
):
    mixed = first_ref[...] + second_ref[...]
    width, samples = mixed.shape

    def by_task(x):
        return x.reshape(tasks, width // tasks, samples)

    inner = mixed + bias_ref[...]
    upper = gelu(inner)
    keep = keep_ref[...]
    targets = target_ref[...]
    score = jnp.sum(by_task(upper * out_ref[...]), axis=1) + last_ref[...]
    faded = jnp.exp(-jnp.abs(score))
    softplus = jnp.maximum(score, 0.0) + jnp.log1p(faded)
    sigmoid = jnp.where(score >= 0.0, 1.0, faded) / (1.0 + faded)
    d_score = keep * (sigmoid - targets) / total_ref[0]
    wide = jnp.broadcast_to(d_score[:, None, :], by_task(mixed).shape).reshape(width, samples)
    d_inner = wide * out_ref[...] * gelu_slope(inner)
    packed_ref[:width, :] = d_inner
    mean = jnp.sum(by_task(d_inner * mixed), axis=1)
    packed_ref[width:, :] = jnp.concatenate(
        [mean, jnp.zeros((packed_ref.shape[0] - width - tasks, samples), jnp.float32)], axis=0
    )
    grad_out_ref[...] = jnp.sum(wide * upper, axis=1, keepdims=True)
    grad_bias_ref[...] = jnp.sum(d_inner, axis=1, keepdims=True)
    small_ref[0] = jnp.sum(d_score, axis=1, keepdims=True)
    small_ref[1] = jnp.sum(keep * (softplus - targets * score), axis=1, keepdims=True)


def score_step(tasks, weight_total, first, second, bias, out, last, keep, targets, before):
    width, samples = first.shape
    shapes = [(-(-(width + tasks) // 8) * 8, samples), (width, 1), (width, 1), (2, tasks, 1)]
    return pl.pallas_call(
        functools.partial(score_kernel, tasks),
        out_shape=[jax.ShapeDtypeStruct(shape, jnp.float32) for shape in shapes],
        in_specs=[SCALARS] + [WHOLE] * 7 + [ANYWHERE],
        out_specs=[WHOLE] * 4,
        compiler_params=pltpu.CompilerParams(vmem_limit_bytes=8 * MIB),
    )(weight_total, first, second, bias, out, last, keep, targets, before)


def backward_kernel(dims, place, member_ref, peer_ref, *refs):
    tasks, experts, mine, hidden_units, tower_units = dims
    stripe, spot = place
    width = tasks * tower_units
    packed_refs, prob_ref, (tower_high, tower_low, gate_high, gate_low), far_in = (
        refs[:2],
        refs[2],
        refs[3:7],
        refs[7:11],
    )
    far_out, (logit_ref, near_ref, far_ref), refs = refs[11:15], refs[15:18], refs[18:]
    pre, upper, weight, d_pre, spreads, (in_sem, out_sem) = (
        refs[0],
        refs[1],
        refs[2:4],
        refs[4:6],
        refs[6:8],
        refs[8:],
    )
    loads = [
        pltpu.make_async_copy(a, b, in_sem.at[k])
        for k, (a, b) in enumerate(zip(far_in, [upper, pre, *weight]))
    ]
    for load in loads:
        load.start()
    stores = [
        pltpu.make_async_copy(a, b, out_sem.at[k])
        for k, (a, b) in enumerate(zip([*d_pre, *spreads], far_out))
    ]
    total = 2 * LANES
    packed = jnp.concatenate([ref[...] for ref in packed_refs], axis=1)
    d_inner = packed[:width].reshape(tasks, tower_units, total)
    mean = packed[width : width + 8].reshape(1, 8, total)[0][:tasks]
    probs = prob_ref[...].reshape(tasks, experts, total)
    which = lax.broadcasted_iota(jnp.int32, probs.shape, 1)
    d_logits = jnp.zeros(probs.shape, jnp.float32)
    loads[0].wait()
    for i in range(mine):
        chosen = which == member_ref[0] * mine + i
        own = jnp.sum(jnp.where(chosen, probs, 0.0), axis=1, keepdims=True)
        d_prob = jnp.sum(d_inner * upper[i].reshape(d_inner.shape), axis=1)
        d_logit = own * (d_prob - mean)[:, None, :]
        d_logits = jnp.where(chosen, d_logit, d_logits)
        value = split((d_inner * own).reshape(width, total))
        spreads[0][i], spreads[1][i] = value
        if i == 0:
            loads[1].wait()
        at = slice(i * hidden_units, (i + 1) * hidden_units)
        d_hidden = product([tower_high[...], tower_low[...]], value)
        value = d_hidden * gelu_slope(pre[at, :])
        d_pre[0][at, :], d_pre[1][at, :] = split(value)
    for store in stores:
        store.start()
    d_logits = d_logits.reshape(tasks * experts, total)
    d_logits = jnp.concatenate(
        [d_logits, jnp.zeros((GATE_LANES - tasks * experts, total), jnp.float32)], axis=0
    )
    logit_ref[...] = d_logits
    d_logits = split(d_logits)
    for k in range(2, 4):
        loads[k].wait()
    tile = 256

    def rows(i, carry):
        at = pl.ds(pl.multiple_of(i * tile, tile), tile)
        value = product([w[at, :] for w in weight], [d_pre[0][...], d_pre[1][...]])
        value = value + product([gate_high[at, :], gate_low[at, :]], d_logits)
        for k in range(tile // stripe):
            to = pl.ds(
                pl.multiple_of(spot(i * (tile // stripe) + k, peer_ref[0]) * stripe, stripe),
                stripe,
            )
            near_ref[to, :] = value[k * stripe : (k + 1) * stripe, :LANES]
            far_ref[to, :] = value[k * stripe : (k + 1) * stripe, LANES:]
        return carry

    lax.fori_loop(0, near_ref.shape[0] // tile, rows, 0)
    for store in stores:
        store.wait()


def backward(dims, place, member, peer, packed, pre, probs, upper, weight, tower, gate):
    tasks, experts, mine, hidden_units, tower_units = dims
    lots = mine * hidden_units
    width = tasks * tower_units
    depth = weight[0].shape[0]
    total = 2 * LANES
    far = [((lots, total), jnp.bfloat16)] * 2 + [((mine, width, total), jnp.bfloat16)] * 2
    near = [
        ((GATE_LANES, total), jnp.float32),
        ((depth, LANES), jnp.float32),
        ((depth, LANES), jnp.float32),
    ]
    return pl.pallas_call(
        functools.partial(backward_kernel, dims, place),
        out_shape=[jax.ShapeDtypeStruct(*x) for x in far + near],
        in_specs=[SCALARS, SCALARS] + [WHOLE] * 7 + [FAR] * 4,
        out_specs=[FAR] * 4 + [WHOLE] * 3,
        scratch_shapes=[pltpu.VMEM(pre.shape, jnp.float32), pltpu.VMEM(upper.shape, jnp.float32)]
        + [pltpu.VMEM(weight[0].shape, jnp.bfloat16)] * 2
        + [pltpu.VMEM(*x) for x in far]
        + [pltpu.SemaphoreType.DMA((4,))] * 2,
        compiler_params=pltpu.CompilerParams(vmem_limit_bytes=ROOM),
        cost_estimate=pl.CostEstimate(
            flops=8 * lots * depth * total, bytes_accessed=12 * MIB, transcendentals=lots * total
        ),
    )(member, peer, *packed, probs, *tower, *gate, upper, pre, *weight)


def gradient_kernel(dims, depth, tower_depth, order, outs, befores, peer_ref, *refs):
    mine, hidden_units = dims
    logits, sources, refs = refs[:2], refs[2:18], refs[18 + befores :]
    weight_refs, bias_ref, refs = refs[:outs], refs[outs], refs[outs + 1 :]
    far_refs = weight_refs
    x, d_pre, hid, spreads = refs[:2], refs[2:4], refs[4:6], refs[6:8]
    weight_refs, (tower, in_sem, out_sem) = refs[8 : 8 + outs], refs[8 + outs :]
    half = 2 * LANES
    places = [
        pair[k].at[(Ellipsis, pl.ds(h * half, half))] if pair is not spreads else pair[k].at[h]
        for pair in (x, d_pre, hid, spreads)
        for h in range(2)
        for k in range(2)
    ]
    loads = [pltpu.make_async_copy(sources[k], places[k], in_sem.at[k]) for k in range(16)]
    for load in loads:
        load.start()
    lots = d_pre[0].shape[0]
    tile = LANES
    share = tile // depth
    tiles = x[0].shape[0] // tile
    gate_at = -(-tower_depth // 8) * TOWER_LANES
    gate_end = gate_at + depth // 8 * GATE_LANES
    for load in loads[:8]:
        load.wait()

    def parts(i):
        if outs == 1:
            return [(weight_refs[0], (), i * share, share)]
        high, middle, low = i // 4, i // 2 % 2, i % 2
        return [(weight_refs[low], (middle, high), 0, 2), (weight_refs[2 + middle], (low, high), 0, 2)]

    wide = 256
    body, tail = slice(0, depth), slice(depth, depth + 8)

    def stores(rows, lanes, n):
        at = (Ellipsis, rows, lanes)
        return [
            pltpu.make_async_copy(a.at[at], b.at[at], out_sem.at[n, k])
            for k, (a, b) in enumerate(zip(weight_refs, far_refs))
        ]

    def columns(n, carry):
        at = pl.ds(pl.multiple_of(n * wide, wide), wide)
        value = product([x[0][...], x[1][...]], [d[at, :] for d in d_pre], True)
        ones = jnp.ones((8, x[0].shape[1]), jnp.bfloat16)
        bias_ref[:, at] = sum(
            lax.dot_general(
                ones, d[at, :], (((1,), (1,)), ((), ())), preferred_element_type=jnp.float32
            )
            for d in d_pre
        )
        for i in range(tiles):
            row = i * tile
            for ref, where, first, many in parts(i):
                ref[(*where, slice(first, first + many), slice(0, depth), at)] = value[
                    row : row + many * depth
                ].reshape(many, depth, wide)
                row += many * depth
        for store in stores(body, at, n):
            store.start()
        return carry

    lax.fori_loop(0, lots // wide, columns, 0)
    d_logits = split(jnp.concatenate([ref[...] for ref in logits], axis=1))
    gates = product([x[0][...], x[1][...]], d_logits, True)
    for load in loads[8:]:
        load.wait()
    value = None
    for i in range(mine):
        for k in range(2):
            at = (slice(i * hidden_units, (i + 1) * hidden_units), slice(k * half, (k + 1) * half))
            part = product([h[at] for h in hid], [p[k, i] for p in spreads], True)
            value = part if value is None else value + part
    tower[...] = jnp.concatenate(
        [value, jnp.zeros((value.shape[0], TOWER_LANES - value.shape[1]), jnp.float32)], axis=1
    )
    full = gate_end == lots and tower_depth % 8 == 0
    for i in range(tiles):
        d = i * share
        for ref, where, first, many in parts(i):
            for k in range(first, first + many):
                if not full:
                    ref[(*where, k, slice(depth, depth + 8), slice(None))] = jnp.zeros(
                        (8, lots), jnp.float32
                    )
                row = tower_row(order, peer_ref, d // 4, d % 4, tower_depth)
                for j in range(0, tower_depth, 8):
                    high = min(8, tower_depth)
                    to = j // 8 * TOWER_LANES
                    ref[(*where, k, slice(depth, depth + high), slice(to, to + TOWER_LANES))] = (
                        tower[pl.ds(row + j, high), :]
                    )
                eights = [gates[d * depth + j : d * depth + j + 8] for j in range(0, depth, 8)]
                ref[(*where, k, slice(depth, depth + 8), slice(gate_at, gate_end))] = (
                    jnp.concatenate(eights, axis=1) if len(eights) > 1 else eights[0]
                )
                d += 1
    for store in stores(tail, slice(None), lots // wide):
        store.start()
    for n in range(lots // wide):
        for store in stores(body, slice(n * wide, (n + 1) * wide), n):
            store.wait()
    for store in stores(tail, slice(None), lots // wide):
        store.wait()


def gradients(dims, devices, depth, tower_depth, order, peer, logits, operands, before):
    mine, hidden_units = dims
    lots = mine * hidden_units
    tall = depth + 8
    counted = order[1]
    shape = (2, 2, 2, tall, lots) if counted else (devices, tall, lots)
    outs = 4 if counted else 1
    total = 4 * LANES
    held = [(devices * depth, total), (lots, total), (lots, total), (2,) + operands[-1].shape]
    return pl.pallas_call(
        functools.partial(
            gradient_kernel, dims, depth, tower_depth, order, outs, len(before)
        ),
        out_shape=[jax.ShapeDtypeStruct(shape, jnp.float32)] * outs
        + [jax.ShapeDtypeStruct((8, lots), jnp.float32)],
        in_specs=[SCALARS, WHOLE, WHOLE] + [FAR] * 16 + [ANYWHERE] * len(before),
        out_specs=[FAR] * outs + [WHOLE],
        scratch_shapes=[pltpu.VMEM(x, jnp.bfloat16) for x in held for _ in range(2)]
        + [pltpu.VMEM(shape, jnp.float32)] * outs
        + [
            pltpu.VMEM((hidden_units, TOWER_LANES), jnp.float32),
            pltpu.SemaphoreType.DMA((16,)),
            pltpu.SemaphoreType.DMA((lots // 256 + 1, outs)),
        ],
        compiler_params=pltpu.CompilerParams(vmem_limit_bytes=ROOM),
        cost_estimate=pl.CostEstimate(
            flops=16 * lots * devices * depth * LANES,
            bytes_accessed=16 * MIB,
            transcendentals=0,
        ),
    )(peer, *logits, *operands, *before)


def swap_near(x):
    count = lax.axis_size("near")
    return lax.ppermute(x, "near", [(i, i ^ 1) for i in range(count)])


def swap_core(x):
    return lax.ppermute(x, "col", [(0, 1), (1, 0)])


def exchange_cores(x, member):
    blocks = [lax.dynamic_index_in_dim(x, member ^ i, 0, False) for i in range(4)]
    return blocks, swap_core(jnp.stack([blocks[1], blocks[3]]))


def exchange_chips(state, member):
    blocks, other = state
    far = swap_near(jnp.stack([blocks[2], other[1]]))
    came = jnp.stack([blocks[0], other[0], far[0], far[1]])
    return jnp.stack([lax.dynamic_index_in_dim(came, member ^ i, 0, False) for i in range(4)])


def exchange_group(x, member, after):
    blocks = [lax.dynamic_index_in_dim(x, member ^ i, 0, False) for i in range(4)]
    came = [
        blocks[0],
        swap_core(blocks[1]),
        swap_near(blocks[2]),
        lax.ppermute(blocks[3], ("near", "col"), [(i, i ^ 3) for i in range(4)]),
    ]
    came = jnp.stack(came)
    member = member + after
    return jnp.stack([lax.dynamic_index_in_dim(came, member ^ i, 0, False) for i in range(4)])


def swap_peer(x, bit):
    if bit == 4:
        return lax.ppermute(x, "hi", [(0, 1), (1, 0)])
    return lax.ppermute(x, "rest", [(i, i ^ bit) for i in range(lax.axis_size("rest"))])


def near_peers(x):
    return [swap_peer(x, bit) for bit in (1, 2, 4)]


def gather_plane(own, one, two):
    cut = own.shape[0] // 2
    return [own, one, two, swap_peer(two[:cut], 1), swap_peer(one[cut:], 2)]


def both_sums(x, far, axis):
    return [
        lax.index_in_dim(x, i, axis, False) + lax.index_in_dim(far, i, axis, False)
        for i in range(2)
    ]


def padded(x, width):
    return jnp.pad(x, [(0, 0)] * (x.ndim - 1) + [(0, width - x.shape[-1])])


def per_device(
    tables,
    table_moment,
    table_square,
    expert_weight,
    expert_moment,
    expert_square,
    gate_weight,
    gate_moment,
    gate_square,
    tower_weight,
    tower_moment,
    tower_square,
    expert_bias,
    bias_moment,
    bias_square,
    head_bias,
    head_moment,
    head_square,
    tower_output,
    output_moment,
    output_square,
    lookup_ids,
    bag_lengths,
    sample_counts,
    labels,
    label_mask,
    sample_weight,
):
    halves = lax.axis_size("col")
    rest = lax.axis_size("rest")
    pieces = 4 * rest
    devices = pieces * halves
    groups = 2 * rest
    members = devices // groups
    rows_here, width_here = tables.shape
    tabs_here = width_here // DIM
    samples, tabs, bag = lookup_ids.shape
    each = samples * bag // pieces
    classes = pieces // bag
    experts, depth, hidden_units = expert_weight.shape
    mine = experts // members
    tasks, tower_depth, tower_units = tower_weight.shape
    upper_width = tasks * tower_units
    member = lax.axis_index("near") * halves + lax.axis_index("col")
    counted = groups == 8
    peer = lax.axis_index("hi") * rest + lax.axis_index("rest") if counted else jnp.int32(0)
    peer_at = peer.astype(jnp.int32).reshape(1)
    depth = expert_weight.shape[1]

    def spot(stripe, own):
        high, near, low = stripe // (2 * rest), stripe // rest % 2, stripe % rest
        return ((high * rest + low) ^ own) * 2 + near

    def natural(stripe, own):
        number, near = (stripe // 2) ^ own, stripe % 2
        return (number // rest * 2 + near) * rest + number % rest

    place = (halves * depth, spot)
    place_back = (halves * depth, natural)

    order = (rest, counted)

    def reorder(x):
        return x.reshape((each, classes) + x.shape[1:]).swapaxes(0, 1).reshape(x.shape)

    live = (jnp.arange(samples, dtype=jnp.int32) < sample_counts[0]).astype(jnp.float32)
    keep = reorder(sample_weight[:, None] * label_mask.astype(jnp.float32) * live[:, None])
    targets = reorder(labels.astype(jnp.float32))

    ids = lookup_ids.transpose(0, 2, 1).reshape(each, pieces, tabs)
    use = jnp.arange(bag, dtype=jnp.int32)[None, :, None] < bag_lengths[:, None, :]
    owner = ids // rows_here
    local = jnp.where(use.reshape(each, pieces, tabs), ids - owner * rows_here, rows_here)
    here = owner[None] == jnp.arange(pieces, dtype=jnp.int32)[:, None, None, None]
    wanted = jnp.sum(jnp.where(here, local[None], 0), axis=2)
    wanted = wanted.transpose(0, 2, 1).reshape(devices, tabs_here * each).astype(jnp.float32)
    message = jnp.concatenate(
        [wanted, jnp.broadcast_to(jnp.sum(keep), (devices, 1))], axis=1
    )
    wide = -(-message.shape[1] // 1024) * 1024
    message = padded(message, wide).reshape(devices, wide // LANES, LANES)
    shifts = lookup_ids[0, :, 0] // rows_here

    lots = mine * hidden_units
    send = expert_weight.reshape(members, mine, depth, hidden_units).swapaxes(1, 2)
    send = send.reshape(members, depth, lots)
    small = pack_rows(
        tower_weight.swapaxes(0, 1).reshape(tower_depth, upper_width),
        gate_weight.swapaxes(0, 1).reshape(depth, tasks * experts),
        lots,
    )
    send = jnp.concatenate(
        [send, jnp.broadcast_to(small[None], (members,) + small.shape)], axis=1
    )
    asked = lax.all_to_all(message, ALL, 0, 0, tiled=True).reshape(devices, wide)
    idx = asked[:, : tabs_here * each].reshape(devices, tabs_here, each)
    idx = idx.swapaxes(0, 1).reshape(-1).astype(jnp.int32)
    weight_total = jnp.sum(asked[:, tabs_here * each])

    shared = exchange_group(send, member, jnp.minimum(idx[0], 0))
    if counted:
        one, two, top = near_peers(shared)
        parts = gather_plane(shared, one, two)
        early = [one, two, top]
        parts += gather_plane(top, swap_peer(top, 1), swap_peer(top, 2))
    else:
        early = [shared]
        parts = [lax.all_gather(shared, PEERS, axis=0, tiled=True)]
    bias_mine = lax.dynamic_slice_in_dim(expert_bias, member * mine, mine, 0).reshape(lots, 1)

    picked = fence(gather_rows(idx, tables, devices, each), early, ROOM)
    cols = width_here // LANES
    arrived = lax.all_to_all(
        picked.reshape(devices, cols * each, LANES), ALL, 0, 0, tiled=True
    ).reshape(pieces, halves, cols, each, LANES)
    def pairs(turn, before):
        return split_weights(
            parts, peer_at, order, depth, tower_depth, upper_width, turn, before
        )

    weight_turned, tower_turned, gate_turned = pairs(True, [])
    mine_x = pool(shifts, peer_at, place, arrived, parts)
    near_x = swap_near(mine_x)
    halves_x = [(mine_x, swap_core(mine_x))]

    dims = (tasks, experts, mine, hidden_units, tower_units)
    member_at = member.astype(jnp.int32).reshape(1)
    def half_forward(x):
        return forward(
            dims, member_at, x, weight_turned, tower_turned, gate_turned, bias_mine
        )

    runs = [half_forward(halves_x[0])]
    near_x = fence(near_x, [runs[0][7]])
    halves_x.append((near_x, swap_core(near_x)))
    runs.append(half_forward(halves_x[1]))
    part_own, part_near = runs[0][7], runs[1][7]
    weight_pair, tower_pair, gate_pair = pairs(False, [part_near])
    first = part_own[0] + swap_core(part_own[1])
    second = swap_near(part_near[0] + swap_core(part_near[1]))
    packed, grad_output, grad_head, few = score_step(
        tasks,
        weight_total.reshape(1),
        first,
        second,
        head_bias[:, :-1].reshape(upper_width, 1),
        tower_output.reshape(upper_width, 1),
        head_bias[:, -1:],
        keep.T,
        targets.T,
        gate_pair[0],
    )

    core_packed = swap_core(packed)
    halves_packed = [(packed, core_packed), (swap_near(packed), swap_near(core_packed))]

    def half_back(k, packed):
        run = runs[k]
        return backward(
            dims,
            place_back,
            member_at,
            peer_at,
            packed,
            run[0],
            run[6],
            run[1],
            weight_pair,
            tower_pair,
            gate_pair,
        )

    back = [half_back(0, halves_packed[0])]
    near_first, near_second = halves_packed[1]
    back.append(half_back(1, (fence(near_first, [back[0][4]]), near_second)))
    near_in, far_in = back[1][5:]
    leaving = near_in + swap_core(far_in)

    half_width = width_here
    ahead = jnp.concatenate(
        [leaving[c * half_width : c * half_width + LANES] for c in range(halves)], axis=0
    )
    others = jnp.concatenate(
        [leaving[c * half_width + LANES : (c + 1) * half_width] for c in range(halves)], axis=0
    )
    ahead = swap_near(ahead)
    others = swap_near(fence(others, [ahead], ROOM))
    terms = [back[0][5], swap_core(back[0][6])]

    def starts(first, stride):
        whole = tuple(c * half_width + first for c in range(halves))
        return (whole, whole, tuple(c * stride for c in range(halves)))

    returned = list(
        spread(shifts, terms + [ahead], starts(0, LANES), pieces, halves, cols, 0, 1)
    )
    returned += list(
        spread(
            shifts,
            terms + [fence(others, returned, ROOM)],
            starts(LANES, half_width - LANES),
            pieces,
            halves,
            cols,
            1,
            cols - 1,
        )
    )

    *sums, grad_bias = gradients(
        (mine, hidden_units),
        devices,
        depth,
        tower_depth,
        order,
        peer_at,
        [x[4] for x in back],
        [x[k] for x in runs for k in (2, 3)]
        + [x[k] for x in back for k in (0, 1)]
        + [x[k] for x in runs for k in (4, 5)]
        + [x[k] for x in back for k in (2, 3)],
        [returned[0]],
    )

    grad_head = jnp.concatenate([grad_head.reshape(tasks, tower_units), few[0]], axis=1)
    same = jnp.concatenate(
        [
            grad_bias[0],
            grad_head.reshape(-1),
            grad_output.reshape(-1),
            jnp.sum(few[1]).reshape(1),
        ]
    )
    cuts = [lots, grad_head.size, grad_output.size, 1]
    long = -(-same.shape[0] // 1024) * 1024
    same = jnp.broadcast_to(
        padded(same, long).reshape(1, long // LANES, LANES), (devices, long // LANES, LANES)
    )
    returned[1] = jnp.concatenate([returned[1], same], axis=1)
    came = [lax.all_to_all(x, ALL, 0, 0, tiled=True) for x in returned[:2]]
    new_tables = None
    before = []
    if counted:
        kept = [sums[0], sums[2]]
        far = [swap_peer(sums[1], 1), swap_peer(sums[3], 2)]
    else:
        kept = []
    for u in range(cols):
        later = returned[2:] if u == 0 else []
        new_tables, handed = update_part(
            idx,
            came[u],
            (tables, table_moment, table_square),
            u,
            each,
            new_tables,
            kept + later,
            before,
        )
        kept = handed[: len(kept)]
        if later:
            came += [
                lax.all_to_all(x, ALL, 0, 0, tiled=True) for x in handed[len(handed) - len(later) :]
            ]
        if counted and u == 0:
            a, b = [both_sums(x, y, 0) for x, y in zip(kept, far)]
            kept, before = [a[0], b[0]], [a[1], b[1]]
            far = [swap_peer(a[1], 2), swap_peer(b[1], 1)]
        if counted and u == 1:
            a, b = [both_sums(x, y, 0) for x, y in zip(kept, far)]
            kept, leaves = [[jnp.concatenate([x, y], axis=0)] for x, y in zip(a, b)]
            before = leaves
            far = [swap_peer(leaves[0], 4)]
        if counted and u == 2:
            state = exchange_cores(kept[0] + far[0], member)
            kept, before = [], [state[1]]
    if not counted:
        summed = lax.psum_scatter(sums[0], PEERS, scatter_dimension=0, tiled=True)
        state = exchange_cores(summed, member)
    summed = exchange_chips(state, member)
    shard_experts = (
        summed[:, :depth]
        .reshape(members, depth, mine, hidden_units)
        .swapaxes(1, 2)
        .reshape(experts, depth, hidden_units)
    )
    shard_towers, shard_gates = unpack_rows(
        jnp.sum(summed[:, depth:], axis=0),
        (tower_depth, upper_width),
        (depth, tasks * experts),
    )
    shard_towers = shard_towers.reshape(tower_depth, tasks, tower_units).swapaxes(0, 1)
    shard_gates = shard_gates.reshape(depth, tasks, experts).swapaxes(0, 1)
    same = came[1][:, each:].reshape(devices, long)
    found = []
    start = 0
    for size in cuts:
        found.append(same[:, start : start + size])
        start += size
    summed_bias = jnp.sum(found[0].reshape(2, 2, rest, halves, lots), axis=(0, 2)).reshape(
        experts, hidden_units
    )
    summed_head = jnp.sum(found[1], axis=0).reshape(head_bias.shape)
    summed_output = jnp.sum(found[2], axis=0).reshape(tower_output.shape)
    loss_sum = jnp.sum(found[3])

    return (
        *new_tables,
        *adamw(expert_weight, expert_moment, expert_square, shard_experts, dense_rate),
        *adamw(gate_weight, gate_moment, gate_square, shard_gates, dense_rate),
        *adamw(tower_weight, tower_moment, tower_square, shard_towers, dense_rate),
        *adamw(expert_bias, bias_moment, bias_square, summed_bias, dense_rate),
        *adamw(head_bias, head_moment, head_square, summed_head, dense_rate),
        *adamw(tower_output, output_moment, output_square, summed_output, dense_rate),
        loss_sum,
        weight_total,
    )


def solution(mesh):
    pieces, halves = mesh.devices.shape
    fine = Mesh(mesh.devices.reshape(2, 2, pieces // 4, halves), ALL)
    table = P(ROW, "col")
    middle = P(None, ALL, None)
    first = P(ALL)
    return jax.shard_map(
        per_device,
        mesh=fine,
        in_specs=(table,) * 3 + (middle,) * 9 + (P(),) * 9 + (first,) * 6,
        out_specs=(table,) * 3 + (middle,) * 9 + (P(),) * 11,
        check_vma=False,
    )
```
